32 devices in a mesh: shot: 2 (over x), slab: 16 (over z, y, core).
Axes of the slice: x: 2, y: 2, z: 4, core: 2. Of those that a mesh axis runs over, the one named last changes fastest.
Arguments:
- wavefield: float32 [2, 2, 2048, 2048], P('shot', None, 'slab'), parts along dimension 0, may hold values from -5 to 5
- frequencies: float32 [2], P('shot'), parts along dimension 0, may hold values from 1 to 3
- velocity: float32 [1, 2048, 2048], P(None, 'slab'), may hold values from 1 to 2.25, as said below
- bracket: int32 [1, 2048, 2048], P(None, 'slab'), may hold values from 0 to 1
Outputs:
- propagated: float32 [2, 2, 2048, 2048], P('shot', None, 'slab'), parts along dimension 0
- image: float32 [2, 2048, 2048], P('shot', 'slab'), parts along dimension 0
The draws below stay inside these ranges and needn't reach their ends.
There are 2 independent parts, one for each index of `shot`. The reference program is written for one: setup_inputs(seed, part) draws one part's arguments, and reference() takes and returns one part's arrays. A program takes and returns all parts, laid end to end along the dimension named above; an argument that names none is the same for every part. Nothing has to cross between parts.
Inputs may be any that keep to these rules, and one draw needn't show every extreme that they name: velocity[d, y, x] lies between the reference speeds c_b and c_(b+1) with b = bracket[d, x, y].
All inputs are finite; a program needn't handle non-finite values.
Results may differ from the reference program's by a relative error of at most 0.0003.
Values sent between devices are 32-bit elements; how exact they have to be, the bound alone decides.
A program may use at most 64 MiB of HBM per device.

```python
import math
import jax
import jax.numpy as jnp
from jax import lax

NX = 2048
NY = 2048
NF = 1
DEPTH = 1
NREF = 3


ref_speeds = (1.0, 1.5, 2.25)


def chosen_brackets(key):
    return jax.random.randint(jax.random.fold_in(key, 71), (DEPTH, NX, NY), 0, NREF - 1, dtype=jnp.int32)


def draw_bracket(key, part):
    return chosen_brackets(key)


def draw_velocity(key, part):
    chosen = chosen_brackets(key)
    speeds = jnp.array(ref_speeds, jnp.float32)
    fraction = jax.random.uniform(jax.random.fold_in(key, 72), (DEPTH, NX, NY), jnp.float32)
    lower_speed = speeds[chosen]
    upper_speed = speeds[chosen + 1]
    speed_grid = lower_speed + fraction * (upper_speed - lower_speed)
    return jnp.transpose(speed_grid, (0, 2, 1)).astype(jnp.float32)


def draw_wavefield(key, part):
    grid_shape = (NF, 2, NX, NY)
    values = jnp.clip(jax.random.normal(key, grid_shape, jnp.float32), -5.0, 5.0)
    return values.astype(jnp.float32)


def setup_inputs(seed: int = 0, part: int = 0) -> dict:
    arg_keys = jax.random.split(jax.random.key(seed), 5)
    own_keys = jax.random.split(jax.random.fold_in(arg_keys[4], part), 5)
    wavefield = draw_wavefield(jax.random.fold_in(jax.random.fold_in(arg_keys[4], part), 71), part)
    frequencies = jnp.clip(jnp.exp(jax.random.uniform(own_keys[1], (NF,), jnp.float32, math.log(1.0), math.log(3.0))), 1.0, 3.0)
    velocity = draw_velocity(jax.random.fold_in(arg_keys[4], 71), part)
    bracket = draw_bracket(jax.random.fold_in(arg_keys[4], 71), part)
    return dict(wavefield=wavefield, frequencies=frequencies, velocity=velocity, bracket=bracket)


ref_speeds = (1.0, 1.5, 2.25)
step_length = 1.0

def wavenumbers(extent):
    indices = jnp.arange(extent, dtype=jnp.int32)
    return jnp.minimum(indices, extent - indices).astype(jnp.float32) * (2.0 * math.pi / extent)

def weights(speed_grid, chosen):
    speeds = jnp.array(ref_speeds, jnp.float32)
    lower_speed = jnp.zeros_like(speed_grid)
    upper_speed = jnp.zeros_like(speed_grid)
    for ref_index in range(len(ref_speeds) - 1):
        lower_speed = lower_speed + jnp.where(chosen == ref_index, speeds[ref_index], 0.0)
        upper_speed = upper_speed + jnp.where(chosen == ref_index, speeds[ref_index + 1], 0.0)
    fraction = (speed_grid - lower_speed) / (upper_speed - lower_speed)
    residual_phase = 1.0 / speed_grid - ((1.0 - fraction) / lower_speed + fraction / upper_speed)
    coefficients = []
    for ref_index in range(len(ref_speeds)):
        coefficients.append(jnp.where(chosen == ref_index, 1.0 - fraction, 0.0) + jnp.where(chosen == ref_index - 1, fraction, 0.0))
    return (coefficients, residual_phase)

def reference(wavefield, frequencies, velocity, bracket):
    first_wave = wavenumbers(NX)
    second_wave = wavenumbers(NY)
    wave_square = first_wave[:, None] * first_wave[:, None] + second_wave[None, :] * second_wave[None, :]
    slowness = 1.0 / jnp.array(ref_speeds, jnp.float32)
    speed_rows = jnp.transpose(velocity, (0, 2, 1))
    fields = [lax.complex(wavefield[freq_index, 0], wavefield[freq_index, 1]) for freq_index in range(NF)]
    images = []
    for depth_index in range(DEPTH):
        coefficients, residual_phase = weights(speed_rows[depth_index], bracket[depth_index])
        updated = []
        for freq_index in range(NF):
            angular = frequencies[freq_index]
            spectrum = jnp.fft.fft2(fields[freq_index])
            blended = jnp.zeros_like(spectrum)
            for ref_index in range(NREF):
                wave_number = angular * slowness[ref_index]
                vertical = wave_number * wave_number - wave_square
                root_abs = jnp.sqrt(jnp.abs(vertical))
                real_part = jnp.where(vertical >= 0, jnp.cos(step_length * root_abs), jnp.exp(-step_length * root_abs))
                imag_part = jnp.where(vertical >= 0, jnp.sin(step_length * root_abs), 0.0)
                shifter = lax.complex(real_part, imag_part)
                blended = blended + coefficients[ref_index] * jnp.fft.ifft2(spectrum * shifter)
            angles = angular * step_length * residual_phase
            updated.append(blended * lax.complex(jnp.cos(angles), jnp.sin(angles)))
        fields = updated
        summed = jnp.real(fields[0])
        for freq_index in range(1, NF):
            summed = summed + jnp.real(fields[freq_index])
        images.append(summed)
    propagated = jnp.stack([jnp.stack([jnp.real(field_now), jnp.imag(field_now)]) for field_now in fields])
    return (propagated, jnp.stack(images))
```

```python
import math

import jax
import jax.numpy as jnp
import ml_dtypes
import numpy as np
from jax import lax
from jax.experimental import pallas as pl
from jax.experimental.pallas import tpu as pltpu
from jax.sharding import PartitionSpec as P

ref_speeds = (1.0, 1.5, 2.25)
step_length = 1.0
highest = lax.Precision.HIGHEST


def dft_table(height, breadth, modulus, direction):
    down_index = lax.iota(jnp.int32, height)[:, None]
    across_index = lax.iota(jnp.int32, breadth)[None, :]
    angles = (down_index * across_index % modulus).astype(jnp.float32) * (
        direction * 2.0 * math.pi / modulus
    )
    return (jnp.cos(angles), jnp.sin(angles))


def contract(pattern, left_pair, right_pair):

    def product(one_side, other_side):
        return jnp.einsum(pattern, one_side, other_side, precision=highest)

    return (
        product(left_pair[0], right_pair[0]) - product(left_pair[1], right_pair[1]),
        product(left_pair[0], right_pair[1]) + product(left_pair[1], right_pair[0]),
    )


def rotate(values, factor_pair):
    return (
        values[0] * factor_pair[0] - values[1] * factor_pair[1],
        values[0] * factor_pair[1] + values[1] * factor_pair[0],
    )


def forward_lines(fields):
    item_count, row_count, extent = fields[0].shape
    devices = lax.axis_size("slab")
    line_count = extent // devices
    reshaped = tuple(
        (part_now.reshape(item_count, row_count, line_count, devices) for part_now in fields)
    )
    section_one = contract(
        "nrab,ak->nrkb", reshaped, dft_table(line_count, line_count, line_count, -1.0)
    )
    twisted = rotate(
        section_one,
        tuple((turning[None, None] for turning in dft_table(line_count, devices, extent, -1.0))),
    )
    section_two = contract("nrkb,bq->nkqr", twisted, dft_table(devices, devices, devices, -1.0))
    return tuple(
        (part_now.reshape(item_count, line_count, devices * row_count) for part_now in section_two)
    )


def forward_rows(fields):
    item_count, line_count, extent = fields[0].shape
    devices = lax.axis_size("slab")
    row_count = extent // devices
    reshaped = tuple(
        (part_now.reshape(item_count, line_count, devices, row_count) for part_now in fields)
    )
    section_one = contract("ncab,ak->nckb", reshaped, dft_table(devices, devices, devices, -1.0))
    twisted = rotate(
        section_one,
        tuple((turning[None, None] for turning in dft_table(devices, row_count, extent, -1.0))),
    )
    section_two = contract(
        "nckb,bq->nckq", twisted, dft_table(row_count, row_count, row_count, -1.0)
    )
    return tuple((part_now.reshape(item_count, line_count, extent) for part_now in section_two))


def inverse_rows(fields):
    item_count, line_count, extent = fields[0].shape
    devices = lax.axis_size("slab")
    row_count = extent // devices
    reshaped = tuple(
        (part_now.reshape(item_count, line_count, devices, row_count) for part_now in fields)
    )
    section_one = contract(
        "nckq,bq->nckb", reshaped, dft_table(row_count, row_count, row_count, 1.0)
    )
    twisted = rotate(
        section_one,
        tuple((turning[None, None] for turning in dft_table(devices, row_count, extent, 1.0))),
    )
    section_two = contract("nckb,ak->ncab", twisted, dft_table(devices, devices, devices, 1.0))
    return tuple(
        (
            part_now.reshape(item_count, line_count, extent) * (1.0 / extent)
            for part_now in section_two
        )
    )


def inverse_lines(fields):
    item_count, line_count, extent = fields[0].shape
    devices = lax.axis_size("slab")
    row_count = extent // devices
    total_lines = line_count * devices
    reshaped = tuple(
        (part_now.reshape(item_count, line_count, devices, row_count) for part_now in fields)
    )
    section_one = contract("nkqr,bq->nkbr", reshaped, dft_table(devices, devices, devices, 1.0))
    twisted = rotate(
        section_one,
        tuple(
            (
                turning[None, :, :, None]
                for turning in dft_table(line_count, devices, total_lines, 1.0)
            )
        ),
    )
    section_two = contract(
        "nkbr,ak->nrab", twisted, dft_table(line_count, line_count, line_count, 1.0)
    )
    return tuple(
        (
            part_now.reshape(item_count, row_count, total_lines) * (1.0 / total_lines)
            for part_now in section_two
        )
    )


def phase_shift(values, wave_square, angular):
    slowness = 1.0 / jnp.array(ref_speeds, jnp.float32)
    wave_number = angular[:, None] * slowness[None, :]
    vertical = (wave_number * wave_number)[:, :, None, None] - wave_square[None, None]
    root_abs = jnp.sqrt(jnp.abs(vertical))
    real_part = jnp.where(
        vertical >= 0, jnp.cos(step_length * root_abs), jnp.exp(-step_length * root_abs)
    )
    imag_part = jnp.where(vertical >= 0, jnp.sin(step_length * root_abs), 0.0)
    shifted = rotate((values[0][:, None], values[1][:, None]), (real_part, imag_part))
    item_count = values[0].shape[0]
    return tuple(
        (
            part_now.reshape((item_count * len(ref_speeds),) + values[0].shape[1:])
            for part_now in shifted
        )
    )


def weights(speed_grid, chosen):
    speeds = jnp.array(ref_speeds, jnp.float32)
    lower_speed = jnp.zeros_like(speed_grid)
    upper_speed = jnp.zeros_like(speed_grid)
    for ref_index in range(len(ref_speeds) - 1):
        lower_speed = lower_speed + jnp.where(chosen == ref_index, speeds[ref_index], 0.0)
        upper_speed = upper_speed + jnp.where(chosen == ref_index, speeds[ref_index + 1], 0.0)
    fraction = (speed_grid - lower_speed) / (upper_speed - lower_speed)
    residual_phase = 1.0 / speed_grid - ((1.0 - fraction) / lower_speed + fraction / upper_speed)
    coefficients = []
    for ref_index in range(len(ref_speeds)):
        coefficients.append(
            jnp.where(chosen == ref_index, 1.0 - fraction, 0.0)
            + jnp.where(chosen == ref_index - 1, fraction, 0.0)
        )
    return (jnp.stack(coefficients), residual_phase)


def advance(fields, angular, coefficients, residual_phase, spec_square):
    item_count, row_count, extent = fields[0].shape
    prepared = forward_lines(fields)
    spectrum = forward_rows(
        (
            lax.all_to_all(prepared[0], "slab", split_axis=2, concat_axis=2, tiled=True),
            lax.all_to_all(prepared[1], "slab", split_axis=2, concat_axis=2, tiled=True),
        )
    )
    returned = inverse_rows(phase_shift(spectrum, spec_square, angular))
    waves = inverse_lines(
        (
            lax.all_to_all(returned[0], "slab", split_axis=2, concat_axis=2, tiled=True),
            lax.all_to_all(returned[1], "slab", split_axis=2, concat_axis=2, tiled=True),
        )
    )
    ref_count = len(ref_speeds)
    wave_real = waves[0].reshape(item_count, ref_count, row_count, extent)
    wave_imag = waves[1].reshape(item_count, ref_count, row_count, extent)
    blended_real = jnp.sum(coefficients[None] * wave_real, axis=1)
    blended_imag = jnp.sum(coefficients[None] * wave_imag, axis=1)
    angles = angular[:, None, None] * step_length * residual_phase[None]
    return rotate((blended_real, blended_imag), (jnp.cos(angles), jnp.sin(angles)))


def folded(indices, modulus):
    return jnp.minimum(indices, modulus - indices).astype(jnp.float32) * (2.0 * math.pi / modulus)


def per_device(wavefield, frequencies, velocity, bracket):
    devices = lax.axis_size("slab")
    device_index = lax.axis_index("slab")
    row_count = wavefield.shape[2]
    extent_y = wavefield.shape[3]
    extent_x = row_count * devices
    line_count = extent_y // devices
    speed_columns = lax.all_to_all(velocity, "slab", split_axis=2, concat_axis=1, tiled=True)
    speed_rows = jnp.transpose(speed_columns, (0, 2, 1))
    column = lax.iota(jnp.int32, extent_x)
    line_index = lax.iota(jnp.int32, line_count)
    spec_first = folded(column // row_count + devices * (column % row_count), extent_x)
    spec_second = folded(device_index * line_count + line_index, extent_y)
    spec_square = (
        spec_first[None, :] * spec_first[None, :] + spec_second[:, None] * spec_second[:, None]
    )
    current = (wavefield[:, 0], wavefield[:, 1])
    coefficients, residual_phase = weights(speed_rows[0], bracket[0])
    single = (current[0], current[1])
    pieces = [advance(single, frequencies, coefficients, residual_phase, spec_square)]
    current = (
        jnp.concatenate([piece[0] for piece in pieces], axis=0),
        jnp.concatenate([piece[1] for piece in pieces], axis=0),
    )
    image_rows = [jnp.sum(current[0], axis=0)]
    return (jnp.stack(current, axis=1), jnp.stack(image_rows))


lanes = 128
chunk = 8
bfloat = jnp.bfloat16
phase_degree = 9


def split_tables(devices):
    extent = devices * lanes
    block = np.arange(devices)[:, None, None]
    down = np.arange(lanes)[None, :, None]
    across = np.arange(lanes)[None, None, :]
    angles = (down * (block + devices * across) % extent) * (2.0 * math.pi / extent)
    cosine, sine = np.cos(angles), np.sin(angles)
    table = np.concatenate(
        [np.concatenate([cosine, -sine], 2), np.concatenate([sine, cosine], 2)], 1
    ).astype(np.float32)
    pieces = []
    for whole in (table, np.ascontiguousarray(np.swapaxes(table, 1, 2))):
        high = whole.astype(ml_dtypes.bfloat16)
        pieces += [high, (whole - high.astype(np.float32)).astype(ml_dtypes.bfloat16)]
    return pieces


def phase_series():
    top = 9.1
    nodes = 0.5 * top * (1.0 + np.cos(math.pi * (np.arange(64) + 0.5) / 64))
    root = np.sqrt(nodes)
    out = []
    for values in (np.cos(root), np.sin(root) / root):
        fit = np.polynomial.chebyshev.Chebyshev.fit(nodes, values, phase_degree, domain=[0, top])
        out.append([float(c) for c in fit.convert(kind=np.polynomial.Polynomial).coef])
    return out


def horner(coefficients, u):
    total = jnp.full_like(u, coefficients[-1])
    for c in coefficients[-2::-1]:
        total = total * u + c
    return total


def halves(values):
    high = values.astype(bfloat)
    return high, (values - high.astype(jnp.float32)).astype(bfloat)


def dot(left, right):
    return jnp.dot(left, right, preferred_element_type=jnp.float32)


def dot_right(values, high, low):
    top, rest = halves(values)
    return dot(top, high) + (dot(rest, high) + dot(top, low))


def dot_left(high, low, values):
    top, rest = halves(values)
    return dot(high, top) + (dot(high, rest) + dot(low, top))


def butterflies(values, sign):
    count = len(values)
    if count == 1:
        return values
    even = butterflies(values[0::2], sign)
    odd = butterflies(values[1::2], sign)
    half = count // 2
    first, second = [], []
    for k in range(half):
        re, im = odd[k]
        if k == 0:
            pass
        elif 4 * k == count:
            re, im = -sign * im, sign * re
        elif 8 * k == count:
            h = math.sqrt(0.5)
            re, im = h * (re - sign * im), h * (im + sign * re)
        elif 8 * k == 3 * count:
            h = math.sqrt(0.5)
            re, im = -h * (re + sign * im), h * (sign * re - im)
        else:
            c = math.cos(2.0 * math.pi * k / count)
            s = sign * math.sin(2.0 * math.pi * k / count)
            re, im = c * re - s * im, c * im + s * re
        er, ei = even[k]
        first.append((er + re, ei + im))
        second.append((er - re, ei - im))
    return first + second


def migrate_kernel(
    devices,
    wave_ref, freq_ref, vel_ref, bracket_ref, ah_ref, al_ref, th_ref, tl_ref,
    out_ref, image_ref,
    lines, sends, spec, factors, parts, waves, speed_recv, coef, turn,
    send_f, recv_f, send_v, recv_v, send_p, recv_p,
):
    me = lax.axis_index("slab")
    refs = len(ref_speeds)
    steps = lanes // chunk
    extent = devices * lanes
    cos_series, sin_series = phase_series()

    def forward_copy(target, block):
        return pltpu.make_async_remote_copy(
            src_ref=sends.at[target], dst_ref=spec.at[block],
            send_sem=send_f.at[target], recv_sem=recv_f.at[block],
            device_id={"slab": target}, device_id_type=pl.DeviceIdType.MESH,
        )

    def speed_copy(target, block):
        return pltpu.make_async_remote_copy(
            src_ref=vel_ref.at[0, :, pl.ds(pl.multiple_of(target * lanes, lanes), lanes)],
            dst_ref=speed_recv.at[block],
            send_sem=send_v.at[target], recv_sem=recv_v.at[block],
            device_id={"slab": target}, device_id_type=pl.DeviceIdType.MESH,
        )

    def part_copy(j, target, block):
        return pltpu.make_async_remote_copy(
            src_ref=parts.at[j, target], dst_ref=waves.at[j, block],
            send_sem=send_p.at[j, target], recv_sem=recv_p.at[j, block],
            device_id={"slab": target}, device_id_type=pl.DeviceIdType.MESH,
        )

    def peer(step):
        return lax.rem(me + step, devices)

    def origin(step):
        return lax.rem(me + devices - step, devices)

    barrier = pltpu.get_barrier_semaphore()

    @pl.loop(1, devices)
    def _(step):
        pl.semaphore_signal(
            barrier, inc=1, device_id={"slab": peer(step)}, device_id_type=pl.DeviceIdType.MESH
        )

    @pl.loop(0, steps)
    def _(i):
        rows = pl.ds(pl.multiple_of(i * chunk, chunk), chunk)
        values = [
            (
                wave_ref[0, 0, rows, a * lanes : (a + 1) * lanes],
                wave_ref[0, 1, rows, a * lanes : (a + 1) * lanes],
            )
            for a in range(devices)
        ]
        for k, (re, im) in enumerate(butterflies(values, -1.0)):
            lines[k, rows, :lanes] = re
            lines[k, rows, lanes:] = im

    pl.semaphore_wait(barrier, devices - 1)

    @pl.loop(1, devices)
    def _(step):
        k = peer(step)
        got = dot_right(lines[k], ah_ref[k], al_ref[k])
        sends[k, :lanes, :] = got[:, :lanes]
        sends[k, lanes:, :] = got[:, lanes:]
        forward_copy(k, me).start()

    got = dot_right(lines[me], ah_ref[me], al_ref[me])
    spec[me, :lanes, :] = got[:, :lanes]
    spec[me, lanes:, :] = got[:, lanes:]

    @pl.loop(1, devices)
    def _(step):
        speed_copy(peer(step), me).start()

    angular = freq_ref[0]
    unit = 2.0 * math.pi / extent
    tall = 4 * chunk
    line_index = me + devices * lax.broadcasted_iota(jnp.int32, (tall, lanes), 1)
    second = jnp.minimum(line_index, extent - line_index).astype(jnp.float32) * unit
    second_square = second * second
    row_iota = lax.broadcasted_iota(jnp.int32, (tall, lanes), 0)
    scale = 1.0 / (extent * extent)

    @pl.loop(0, devices)
    def _(k):
        @pl.loop(0, lanes // tall)
        def _(i):
            start = pl.multiple_of(i * tall, tall)
            column = k + devices * (row_iota + start)
            first = jnp.minimum(column, extent - column).astype(jnp.float32) * unit
            square = first * first + second_square
            for j, speed in enumerate(ref_speeds):
                number = angular * np.float32(1.0 / speed)
                vertical = number * number - square
                root = jnp.sqrt(jnp.abs(vertical))
                decayed = jnp.exp(-root)
                real = jnp.where(vertical >= 0, horner(cos_series, vertical), decayed)
                imag = jnp.where(vertical >= 0, root * horner(sin_series, vertical), 0.0)
                factors[j, k, pl.ds(start, tall), :] = real * scale
                factors[j, k, pl.ds(start + lanes, tall), :] = imag * scale

    @pl.loop(1, devices)
    def _(step):
        k = origin(step)
        forward_copy(k, k).wait_recv()

    def across(ref, sign):
        @pl.loop(0, steps)
        def _(i):
            top = pl.ds(pl.multiple_of(i * chunk, chunk), chunk)
            low = pl.ds(pl.multiple_of(i * chunk + lanes, chunk), chunk)
            values = [(ref[d, top, :], ref[d, low, :]) for d in range(devices)]
            for k, (re, im) in enumerate(butterflies(values, sign)):
                ref[k, top, :] = re
                ref[k, low, :] = im

    across(spec, -1.0)

    for j in range(refs):

        @pl.loop(0, devices)
        def _(k):
            if j == 0:
                spec[k] = dot_left(th_ref[k], tl_ref[k], spec[k])
            re, im = spec[k, :lanes, :], spec[k, lanes:, :]
            fr, fi = factors[j, k, :lanes, :], factors[j, k, lanes:, :]
            shifted = jnp.concatenate([re * fr - im * fi, re * fi + im * fr], axis=0)
            parts[j, k] = dot_left(ah_ref[k], al_ref[k], shifted)

        across(parts.at[j], 1.0)

        @pl.loop(1, devices)
        def _(step):
            part_copy(j, peer(step), me).start()

        waves[j, me] = parts[j, me]

    speed_recv[me] = vel_ref[0, :, pl.ds(pl.multiple_of(me * lanes, lanes), lanes)]

    @pl.loop(1, devices)
    def _(step):
        k = origin(step)
        speed_copy(k, k).wait_recv()

    for a in range(devices):
        cols = slice(a * lanes, (a + 1) * lanes)
        speed = speed_recv[a].T
        chosen = bracket_ref[0, :, cols]
        is_low = chosen == 0
        lower = jnp.where(is_low, ref_speeds[0], ref_speeds[1])
        upper = jnp.where(is_low, ref_speeds[1], ref_speeds[2])
        fraction = (speed - lower) / (upper - lower)
        residual = 1.0 / speed - ((1.0 - fraction) / lower + fraction / upper)
        rest = 1.0 - fraction
        coef[0, :, cols] = jnp.where(is_low, rest, 0.0)
        coef[1, :, cols] = jnp.where(is_low, fraction, rest)
        coef[2, :, cols] = jnp.where(is_low, 0.0, fraction)
        angle = angular * step_length * residual
        u = angle * angle
        turn[0, :, cols] = horner([1.0, -1 / 2, 1 / 24, -1 / 720, 1 / 40320], u)
        turn[1, :, cols] = angle * horner([1.0, -1 / 6, 1 / 120, -1 / 5040], u)

    for j in range(refs):

        @pl.loop(0, devices)
        def _(step):
            k = origin(step)

            @pl.when(step > 0)
            def _():
                part_copy(j, k, k).wait_recv()

            row = jnp.concatenate([waves[j, k, :lanes, :], waves[j, k, lanes:, :]], axis=1)
            got = dot_right(row, th_ref[k], tl_ref[k])
            waves[j, k, :lanes, :] = got[:, :lanes]
            waves[j, k, lanes:, :] = got[:, lanes:]

        @pl.loop(0, steps)
        def _(i):
            top = pl.ds(pl.multiple_of(i * chunk, chunk), chunk)
            low = pl.ds(pl.multiple_of(i * chunk + lanes, chunk), chunk)
            values = [(waves[j, k, top, :], waves[j, k, low, :]) for k in range(devices)]
            for a, (re, im) in enumerate(butterflies(values, 1.0)):
                cols = slice(a * lanes, (a + 1) * lanes)
                weight = coef[j, top, cols]
                re, im = re * weight, im * weight
                if j > 0:
                    re = re + out_ref[0, 0, top, cols]
                    im = im + out_ref[0, 1, top, cols]
                if j == refs - 1:
                    c, s = turn[0, top, cols], turn[1, top, cols]
                    re, im = re * c - im * s, re * s + im * c
                    image_ref[0, top, cols] = re
                out_ref[0, 0, top, cols] = re
                out_ref[0, 1, top, cols] = im

    @pl.loop(1, devices)
    def _(step):
        k = peer(step)
        forward_copy(k, me).wait_send()
        speed_copy(k, me).wait_send()
        for j in range(refs):
            part_copy(j, k, me).wait_send()


def migrate(devices, wavefield, frequencies, velocity, bracket):
    refs = len(ref_speeds)
    tables = [jnp.asarray(piece) for piece in split_tables(devices)]
    extent = devices * lanes
    vmem = pl.BlockSpec(memory_space=pltpu.VMEM)
    tall = 2 * lanes
    single = jnp.float32
    return pl.pallas_call(
        lambda *args: migrate_kernel(devices, *args),
        out_shape=(
            jax.ShapeDtypeStruct((1, 2, lanes, extent), single),
            jax.ShapeDtypeStruct((1, lanes, extent), single),
        ),
        in_specs=[vmem, pl.BlockSpec(memory_space=pltpu.SMEM)] + [vmem] * 6,
        out_specs=(vmem, vmem),
        scratch_shapes=[
            pltpu.VMEM((devices, lanes, tall), single),
            pltpu.VMEM((devices, tall, lanes), single),
            pltpu.VMEM((devices, tall, lanes), single),
            pltpu.VMEM((refs, devices, tall, lanes), single),
            pltpu.VMEM((refs, devices, tall, lanes), single),
            pltpu.VMEM((refs, devices, tall, lanes), single),
            pltpu.VMEM((devices, lanes, lanes), single),
            pltpu.VMEM((refs, lanes, extent), single),
            pltpu.VMEM((2, lanes, extent), single),
            pltpu.SemaphoreType.DMA((devices,)),
            pltpu.SemaphoreType.DMA((devices,)),
            pltpu.SemaphoreType.DMA((devices,)),
            pltpu.SemaphoreType.DMA((devices,)),
            pltpu.SemaphoreType.DMA((refs, devices)),
            pltpu.SemaphoreType.DMA((refs, devices)),
        ],
        compiler_params=pltpu.CompilerParams(
            collective_id=0, has_side_effects=True, vmem_limit_bytes=60 * 2**20
        ),
    )(wavefield, frequencies, velocity, bracket, *tables)


def on_device(wavefield, frequencies, velocity, bracket):
    devices = lax.axis_size("slab")
    fits = (
        wavefield.shape[0] == 1
        and velocity.shape[0] == 1
        and wavefield.shape[2] == lanes
        and wavefield.shape[3] == devices * lanes
        and devices in (2, 4, 8, 16)
    )
    if fits:
        return migrate(devices, wavefield, frequencies, velocity, bracket)
    return per_device(wavefield, frequencies, velocity, bracket)


def solution(mesh):
    return jax.shard_map(
        on_device,
        mesh=mesh,
        in_specs=(
            P("shot", None, "slab", None),
            P("shot"),
            P(None, "slab", None),
            P(None, "slab", None),
        ),
        out_specs=(P("shot", None, "slab", None), P("shot", "slab", None)),
        check_vma=False,
    )
```

```python
import math

import jax
import jax.numpy as jnp
import ml_dtypes
import numpy as np
from jax import lax
from jax.experimental import pallas as pl
from jax.experimental.pallas import tpu as pltpu
from jax.sharding import PartitionSpec as P

ref_speeds = (1.0, 1.5, 2.25)
step_length = 1.0
highest = lax.Precision.HIGHEST


def dft_table(height, breadth, modulus, direction):
    down_index = lax.iota(jnp.int32, height)[:, None]
    across_index = lax.iota(jnp.int32, breadth)[None, :]
    angles = (down_index * across_index % modulus).astype(jnp.float32) * (
        direction * 2.0 * math.pi / modulus
    )
    return (jnp.cos(angles), jnp.sin(angles))


def contract(pattern, left_pair, right_pair):

    def product(one_side, other_side):
        return jnp.einsum(pattern, one_side, other_side, precision=highest)

    return (
        product(left_pair[0], right_pair[0]) - product(left_pair[1], right_pair[1]),
        product(left_pair[0], right_pair[1]) + product(left_pair[1], right_pair[0]),
    )


def rotate(values, factor_pair):
    return (
        values[0] * factor_pair[0] - values[1] * factor_pair[1],
        values[0] * factor_pair[1] + values[1] * factor_pair[0],
    )


def forward_lines(fields):
    item_count, row_count, extent = fields[0].shape
    devices = lax.axis_size("slab")
    line_count = extent // devices
    reshaped = tuple(
        (part_now.reshape(item_count, row_count, line_count, devices) for part_now in fields)
    )
    section_one = contract(
        "nrab,ak->nrkb", reshaped, dft_table(line_count, line_count, line_count, -1.0)
    )
    twisted = rotate(
        section_one,
        tuple((turning[None, None] for turning in dft_table(line_count, devices, extent, -1.0))),
    )
    section_two = contract("nrkb,bq->nkqr", twisted, dft_table(devices, devices, devices, -1.0))
    return tuple(
        (part_now.reshape(item_count, line_count, devices * row_count) for part_now in section_two)
    )


def forward_rows(fields):
    item_count, line_count, extent = fields[0].shape
    devices = lax.axis_size("slab")
    row_count = extent // devices
    reshaped = tuple(
        (part_now.reshape(item_count, line_count, devices, row_count) for part_now in fields)
    )
    section_one = contract("ncab,ak->nckb", reshaped, dft_table(devices, devices, devices, -1.0))
    twisted = rotate(
        section_one,
        tuple((turning[None, None] for turning in dft_table(devices, row_count, extent, -1.0))),
    )
    section_two = contract(
        "nckb,bq->nckq", twisted, dft_table(row_count, row_count, row_count, -1.0)
    )
    return tuple((part_now.reshape(item_count, line_count, extent) for part_now in section_two))


def inverse_rows(fields):
    item_count, line_count, extent = fields[0].shape
    devices = lax.axis_size("slab")
    row_count = extent // devices
    reshaped = tuple(
        (part_now.reshape(item_count, line_count, devices, row_count) for part_now in fields)
    )
    section_one = contract(
        "nckq,bq->nckb", reshaped, dft_table(row_count, row_count, row_count, 1.0)
    )
    twisted = rotate(
        section_one,
        tuple((turning[None, None] for turning in dft_table(devices, row_count, extent, 1.0))),
    )
    section_two = contract("nckb,ak->ncab", twisted, dft_table(devices, devices, devices, 1.0))
    return tuple(
        (
            part_now.reshape(item_count, line_count, extent) * (1.0 / extent)
            for part_now in section_two
        )
    )


def inverse_lines(fields):
    item_count, line_count, extent = fields[0].shape
    devices = lax.axis_size("slab")
    row_count = extent // devices
    total_lines = line_count * devices
    reshaped = tuple(
        (part_now.reshape(item_count, line_count, devices, row_count) for part_now in fields)
    )
    section_one = contract("nkqr,bq->nkbr", reshaped, dft_table(devices, devices, devices, 1.0))
    twisted = rotate(
        section_one,
        tuple(
            (
                turning[None, :, :, None]
                for turning in dft_table(line_count, devices, total_lines, 1.0)
            )
        ),
    )
    section_two = contract(
        "nkbr,ak->nrab", twisted, dft_table(line_count, line_count, line_count, 1.0)
    )
    return tuple(
        (
            part_now.reshape(item_count, row_count, total_lines) * (1.0 / total_lines)
            for part_now in section_two
        )
    )


def phase_shift(values, wave_square, angular):
    slowness = 1.0 / jnp.array(ref_speeds, jnp.float32)
    wave_number = angular[:, None] * slowness[None, :]
    vertical = (wave_number * wave_number)[:, :, None, None] - wave_square[None, None]
    root_abs = jnp.sqrt(jnp.abs(vertical))
    real_part = jnp.where(
        vertical >= 0, jnp.cos(step_length * root_abs), jnp.exp(-step_length * root_abs)
    )
    imag_part = jnp.where(vertical >= 0, jnp.sin(step_length * root_abs), 0.0)
    shifted = rotate((values[0][:, None], values[1][:, None]), (real_part, imag_part))
    item_count = values[0].shape[0]
    return tuple(
        (
            part_now.reshape((item_count * len(ref_speeds),) + values[0].shape[1:])
            for part_now in shifted
        )
    )


def weights(speed_grid, chosen):
    speeds = jnp.array(ref_speeds, jnp.float32)
    lower_speed = jnp.zeros_like(speed_grid)
    upper_speed = jnp.zeros_like(speed_grid)
    for ref_index in range(len(ref_speeds) - 1):
        lower_speed = lower_speed + jnp.where(chosen == ref_index, speeds[ref_index], 0.0)
        upper_speed = upper_speed + jnp.where(chosen == ref_index, speeds[ref_index + 1], 0.0)
    fraction = (speed_grid - lower_speed) / (upper_speed - lower_speed)
    residual_phase = 1.0 / speed_grid - ((1.0 - fraction) / lower_speed + fraction / upper_speed)
    coefficients = []
    for ref_index in range(len(ref_speeds)):
        coefficients.append(
            jnp.where(chosen == ref_index, 1.0 - fraction, 0.0)
            + jnp.where(chosen == ref_index - 1, fraction, 0.0)
        )
    return (jnp.stack(coefficients), residual_phase)


def advance(fields, angular, coefficients, residual_phase, spec_square):
    item_count, row_count, extent = fields[0].shape
    prepared = forward_lines(fields)
    spectrum = forward_rows(
        (
            lax.all_to_all(prepared[0], "slab", split_axis=2, concat_axis=2, tiled=True),
            lax.all_to_all(prepared[1], "slab", split_axis=2, concat_axis=2, tiled=True),
        )
    )
    returned = inverse_rows(phase_shift(spectrum, spec_square, angular))
    waves = inverse_lines(
        (
            lax.all_to_all(returned[0], "slab", split_axis=2, concat_axis=2, tiled=True),
            lax.all_to_all(returned[1], "slab", split_axis=2, concat_axis=2, tiled=True),
        )
    )
    ref_count = len(ref_speeds)
    wave_real = waves[0].reshape(item_count, ref_count, row_count, extent)
    wave_imag = waves[1].reshape(item_count, ref_count, row_count, extent)
    blended_real = jnp.sum(coefficients[None] * wave_real, axis=1)
    blended_imag = jnp.sum(coefficients[None] * wave_imag, axis=1)
    angles = angular[:, None, None] * step_length * residual_phase[None]
    return rotate((blended_real, blended_imag), (jnp.cos(angles), jnp.sin(angles)))


def folded(indices, modulus):
    return jnp.minimum(indices, modulus - indices).astype(jnp.float32) * (2.0 * math.pi / modulus)


def per_device(wavefield, frequencies, velocity, bracket):
    devices = lax.axis_size("slab")
    device_index = lax.axis_index("slab")
    row_count = wavefield.shape[2]
    extent_y = wavefield.shape[3]
    extent_x = row_count * devices
    line_count = extent_y // devices
    speed_columns = lax.all_to_all(velocity, "slab", split_axis=2, concat_axis=1, tiled=True)
    speed_rows = jnp.transpose(speed_columns, (0, 2, 1))
    column = lax.iota(jnp.int32, extent_x)
    line_index = lax.iota(jnp.int32, line_count)
    spec_first = folded(column // row_count + devices * (column % row_count), extent_x)
    spec_second = folded(device_index * line_count + line_index, extent_y)
    spec_square = (
        spec_first[None, :] * spec_first[None, :] + spec_second[:, None] * spec_second[:, None]
    )
    current = (wavefield[:, 0], wavefield[:, 1])
    coefficients, residual_phase = weights(speed_rows[0], bracket[0])
    single = (current[0], current[1])
    pieces = [advance(single, frequencies, coefficients, residual_phase, spec_square)]
    current = (
        jnp.concatenate([piece[0] for piece in pieces], axis=0),
        jnp.concatenate([piece[1] for piece in pieces], axis=0),
    )
    image_rows = [jnp.sum(current[0], axis=0)]
    return (jnp.stack(current, axis=1), jnp.stack(image_rows))


lanes = 128
chunk = 8
bfloat = jnp.bfloat16
phase_degree = 9


def split_tables(devices):
    extent = devices * lanes
    block = np.arange(devices)[:, None, None]
    down = np.arange(lanes)[None, :, None]
    across = np.arange(lanes)[None, None, :]
    angles = (down * (block + devices * across) % extent) * (2.0 * math.pi / extent)
    cosine, sine = np.cos(angles), np.sin(angles)
    table = np.concatenate(
        [np.concatenate([cosine, -sine], 2), np.concatenate([sine, cosine], 2)], 1
    ).astype(np.float32)
    pieces = []
    for whole in (table, np.ascontiguousarray(np.swapaxes(table, 1, 2))):
        high = whole.astype(ml_dtypes.bfloat16)
        pieces += [high, (whole - high.astype(np.float32)).astype(ml_dtypes.bfloat16)]
    return pieces


def phase_series():
    top = 9.1
    nodes = 0.5 * top * (1.0 + np.cos(math.pi * (np.arange(64) + 0.5) / 64))
    root = np.sqrt(nodes)
    out = []
    for values in (np.cos(root), np.sin(root) / root):
        fit = np.polynomial.chebyshev.Chebyshev.fit(nodes, values, phase_degree, domain=[0, top])
        out.append([float(c) for c in fit.convert(kind=np.polynomial.Polynomial).coef])
    return out


def horner(coefficients, u):
    total = jnp.full_like(u, coefficients[-1])
    for c in coefficients[-2::-1]:
        total = total * u + c
    return total


def halves(values):
    high = values.astype(bfloat)
    return high, (values - high.astype(jnp.float32)).astype(bfloat)


def dot(left, right):
    return jnp.dot(left, right, preferred_element_type=jnp.float32)


def dot_right(values, high, low):
    top, rest = halves(values)
    return dot(top, high) + (dot(rest, high) + dot(top, low))


def dot_left(high, low, values):
    top, rest = halves(values)
    return dot(high, top) + (dot(high, rest) + dot(low, top))


def turned(value, k, count, sign):
    re, im = value
    h = math.sqrt(0.5)
    if k == 0:
        return re, im
    if 4 * k == count:
        return -sign * im, sign * re
    if 8 * k == count:
        return h * (re - sign * im), h * (im + sign * re)
    if 8 * k == 3 * count:
        return -h * (re + sign * im), h * (sign * re - im)
    c = math.cos(2.0 * math.pi * k / count)
    s = sign * math.sin(2.0 * math.pi * k / count)
    return c * re - s * im, c * im + s * re


def butterflies(values, sign):
    count = len(values)
    if count == 1:
        return values
    even = butterflies(values[0::2], sign)
    odd = butterflies(values[1::2], sign)
    first, second = [], []
    for k in range(count // 2):
        er, ei = even[k]
        re, im = turned(odd[k], k, count, sign)
        first.append((er + re, ei + im))
        second.append((er - re, ei - im))
    return first + second


def half_butterflies(values, sign, side):
    count = len(values)
    even = butterflies(values[0::2], sign)
    odd = butterflies(values[1::2], sign)
    out = []
    for k in range(count // 2):
        er, ei = even[k]
        re, im = turned(odd[k], k, count, sign)
        out.append((er + side * re, ei + side * im))
    return out


def migrate_kernel(
    devices,
    wave_ref, freq_ref, vel_ref, bracket_ref, ah_ref, al_ref, th_ref, tl_ref,
    out_ref, image_ref,
    lines, sends, spec, factors, mixed, parts, waves, speed_recv, coef, turn,
    send_f, recv_f, send_v, recv_v, send_p, recv_p,
):
    me = lax.axis_index("slab")
    refs = len(ref_speeds)
    steps = lanes // chunk
    extent = devices * lanes
    cos_series, sin_series = phase_series()

    half = devices // 2
    place = lax.rem(me, half)
    base = me - place
    other = half - base

    def forward_copy(e, target, block):
        return pltpu.make_async_remote_copy(
            src_ref=sends.at[e * half + lax.rem(target, half)], dst_ref=spec.at[e, block],
            send_sem=send_f.at[e, target], recv_sem=recv_f.at[e, block],
            device_id={"slab": target}, device_id_type=pl.DeviceIdType.MESH,
        )

    def speed_copy(target, block):
        return pltpu.make_async_remote_copy(
            src_ref=vel_ref.at[0, :, pl.ds(pl.multiple_of(target * lanes, lanes), lanes)],
            dst_ref=speed_recv.at[block],
            send_sem=send_v.at[target], recv_sem=recv_v.at[block],
            device_id={"slab": target}, device_id_type=pl.DeviceIdType.MESH,
        )

    def part_copy(j, e, target, block):
        return pltpu.make_async_remote_copy(
            src_ref=parts.at[j, e, target], dst_ref=waves.at[j, e * half + block],
            send_sem=send_p.at[j, e, target], recv_sem=recv_p.at[j, e, block],
            device_id={"slab": base + target}, device_id_type=pl.DeviceIdType.MESH,
        )

    def near(step):
        return lax.rem(place + step, half)

    def near_origin(step):
        return lax.rem(place + half - step, half)

    def peer(step):
        return lax.rem(me + step, devices)

    def origin(step):
        return lax.rem(me + devices - step, devices)

    barrier = pltpu.get_barrier_semaphore()

    @pl.loop(1, devices)
    def _(step):
        pl.semaphore_signal(
            barrier, inc=1, device_id={"slab": peer(step)}, device_id_type=pl.DeviceIdType.MESH
        )

    @pl.loop(0, steps)
    def _(i):
        rows = pl.ds(pl.multiple_of(i * chunk, chunk), chunk)
        values = [
            (
                wave_ref[0, 0, rows, a * lanes : (a + 1) * lanes],
                wave_ref[0, 1, rows, a * lanes : (a + 1) * lanes],
            )
            for a in range(devices)
        ]
        for k, (re, im) in enumerate(butterflies(values, -1.0)):
            lines[k, rows, :lanes] = re
            lines[k, rows, lanes:] = im

    pl.semaphore_wait(barrier, devices - 1)

    for e in range(2):

        @pl.loop(0, half)
        def _(step):
            k = near(step)
            c = e * half + k
            got = dot_right(lines[c], ah_ref[c], al_ref[c])
            sends[c, :lanes, :] = got[:, :lanes]
            sends[c, lanes:, :] = got[:, lanes:]
            forward_copy(e, other + k, me).start()

            @pl.when(step > 0)
            def _():
                forward_copy(e, base + k, me).start()

        spec[e, me] = sends[e * half + place]

    @pl.loop(1, devices)
    def _(step):
        speed_copy(peer(step), me).start()

    angular = freq_ref[0]
    unit = 2.0 * math.pi / extent
    tall = 4 * chunk
    row_iota = lax.broadcasted_iota(jnp.int32, (tall, lanes), 0)
    lane_iota = lax.broadcasted_iota(jnp.int32, (tall, lanes), 1)
    scale = 1.0 / (extent * extent)
    side = (1 - 2 * (base // half)).astype(jnp.float32)

    def make_factors(e):
        line_index = e * half + place + devices * lane_iota
        second = jnp.minimum(line_index, extent - line_index).astype(jnp.float32) * unit
        second_square = second * second

        @pl.loop(0, devices)
        def _(k):
            @pl.loop(0, lanes // tall)
            def _(i):
                start = pl.multiple_of(i * tall, tall)
                column = k + devices * (row_iota + start)
                first = jnp.minimum(column, extent - column).astype(jnp.float32) * unit
                square = first * first + second_square
                for j, speed in enumerate(ref_speeds):
                    number = angular * np.float32(1.0 / speed)
                    vertical = number * number - square
                    root = jnp.sqrt(jnp.abs(vertical))
                    decayed = jnp.exp(-root)
                    real = jnp.where(vertical >= 0, horner(cos_series, vertical), decayed)
                    imag = jnp.where(vertical >= 0, root * horner(sin_series, vertical), 0.0)
                    factors[j, k, pl.ds(start, tall), :] = real * scale
                    factors[j, k, pl.ds(start + lanes, tall), :] = imag * scale

    def across(ref, out, transform):
        @pl.loop(0, steps)
        def _(i):
            top = pl.ds(pl.multiple_of(i * chunk, chunk), chunk)
            low = pl.ds(pl.multiple_of(i * chunk + lanes, chunk), chunk)
            values = [(ref[d, top, :], ref[d, low, :]) for d in range(devices)]
            for k, (re, im) in enumerate(transform(values)):
                out[k, top, :] = re
                out[k, low, :] = im

    for e in range(2):
        make_factors(e)

        @pl.loop(0, half)
        def _(step):
            k = near_origin(step)
            forward_copy(e, other + k, other + k).wait_recv()

            @pl.when(step > 0)
            def _():
                forward_copy(e, base + k, base + k).wait_recv()

        across(spec.at[e], spec.at[e], lambda values: butterflies(values, -1.0))

        for j in range(refs):

            @pl.loop(0, devices)
            def _(k):
                if j == 0:
                    spec[e, k] = dot_left(th_ref[k], tl_ref[k], spec[e, k])
                re, im = spec[e, k, :lanes, :], spec[e, k, lanes:, :]
                fr, fi = factors[j, k, :lanes, :], factors[j, k, lanes:, :]
                shifted = jnp.concatenate([re * fr - im * fi, re * fi + im * fr], axis=0)
                mixed[k] = dot_left(ah_ref[k], al_ref[k], shifted)

            across(mixed, parts.at[j, e], lambda values: half_butterflies(values, 1.0, side))

            @pl.loop(1, half)
            def _(step):
                part_copy(j, e, near(step), place).start()

            waves[j, e * half + place] = parts[j, e, place]

    speed_recv[me] = vel_ref[0, :, pl.ds(pl.multiple_of(me * lanes, lanes), lanes)]

    @pl.loop(1, devices)
    def _(step):
        k = origin(step)
        speed_copy(k, k).wait_recv()

    for a in range(devices):
        cols = slice(a * lanes, (a + 1) * lanes)
        speed = speed_recv[a].T
        chosen = bracket_ref[0, :, cols]
        is_low = chosen == 0
        lower = jnp.where(is_low, ref_speeds[0], ref_speeds[1])
        upper = jnp.where(is_low, ref_speeds[1], ref_speeds[2])
        fraction = (speed - lower) / (upper - lower)
        residual = 1.0 / speed - ((1.0 - fraction) / lower + fraction / upper)
        rest = 1.0 - fraction
        coef[0, :, cols] = jnp.where(is_low, rest, 0.0)
        coef[1, :, cols] = jnp.where(is_low, fraction, rest)
        coef[2, :, cols] = jnp.where(is_low, 0.0, fraction)
        angle = angular * step_length * residual
        u = angle * angle
        turn[0, :, cols] = horner([1.0, -1 / 2, 1 / 24, -1 / 720, 1 / 40320], u)
        turn[1, :, cols] = angle * horner([1.0, -1 / 6, 1 / 120, -1 / 5040], u)

    def receive(j, e):
        @pl.loop(0, half)
        def _(step):
            block = near_origin(step)
            k = e * half + block

            @pl.when(step > 0)
            def _():
                part_copy(j, e, block, block).wait_recv()

            row = jnp.concatenate([waves[j, k, :lanes, :], waves[j, k, lanes:, :]], axis=1)
            got = dot_right(row, th_ref[k], tl_ref[k])
            waves[j, k, :lanes, :] = got[:, :lanes]
            waves[j, k, lanes:, :] = got[:, lanes:]

    for j in range(refs):
        receive(j, 0)

    for j in range(refs):
        receive(j, 1)

        @pl.loop(0, steps)
        def _(i):
            top = pl.ds(pl.multiple_of(i * chunk, chunk), chunk)
            low = pl.ds(pl.multiple_of(i * chunk + lanes, chunk), chunk)
            values = [(waves[j, k, top, :], waves[j, k, low, :]) for k in range(devices)]
            for a, (re, im) in enumerate(butterflies(values, 1.0)):
                cols = slice(a * lanes, (a + 1) * lanes)
                weight = coef[j, top, cols]
                re, im = re * weight, im * weight
                if j > 0:
                    re = re + out_ref[0, 0, top, cols]
                    im = im + out_ref[0, 1, top, cols]
                if j == refs - 1:
                    c, s = turn[0, top, cols], turn[1, top, cols]
                    re, im = re * c - im * s, re * s + im * c
                    image_ref[0, top, cols] = re
                out_ref[0, 0, top, cols] = re
                out_ref[0, 1, top, cols] = im

    @pl.loop(1, devices)
    def _(step):
        speed_copy(peer(step), me).wait_send()

    for e in range(2):

        @pl.loop(0, half)
        def _(step):
            k = near(step)
            forward_copy(e, other + k, me).wait_send()

            @pl.when(step > 0)
            def _():
                forward_copy(e, base + k, me).wait_send()
                for j in range(refs):
                    part_copy(j, e, k, place).wait_send()


def migrate(devices, wavefield, frequencies, velocity, bracket):
    refs = len(ref_speeds)
    tables = [jnp.asarray(piece) for piece in split_tables(devices)]
    extent = devices * lanes
    vmem = pl.BlockSpec(memory_space=pltpu.VMEM)
    half = devices // 2
    tall = 2 * lanes
    single = jnp.float32
    return pl.pallas_call(
        lambda *args: migrate_kernel(devices, *args),
        out_shape=(
            jax.ShapeDtypeStruct((1, 2, lanes, extent), single),
            jax.ShapeDtypeStruct((1, lanes, extent), single),
        ),
        in_specs=[vmem, pl.BlockSpec(memory_space=pltpu.SMEM)] + [vmem] * 6,
        out_specs=(vmem, vmem),
        scratch_shapes=[
            pltpu.VMEM((devices, lanes, tall), single),
            pltpu.VMEM((devices, tall, lanes), single),
            pltpu.VMEM((2, devices, tall, lanes), single),
            pltpu.VMEM((refs, devices, tall, lanes), single),
            pltpu.VMEM((devices, tall, lanes), single),
            pltpu.VMEM((refs, 2, half, tall, lanes), single),
            pltpu.VMEM((refs, devices, tall, lanes), single),
            pltpu.VMEM((devices, lanes, lanes), single),
            pltpu.VMEM((refs, lanes, extent), single),
            pltpu.VMEM((2, lanes, extent), single),
            pltpu.SemaphoreType.DMA((2, devices)),
            pltpu.SemaphoreType.DMA((2, devices)),
            pltpu.SemaphoreType.DMA((devices,)),
            pltpu.SemaphoreType.DMA((devices,)),
            pltpu.SemaphoreType.DMA((refs, 2, half)),
            pltpu.SemaphoreType.DMA((refs, 2, half)),
        ],
        compiler_params=pltpu.CompilerParams(
            collective_id=0, has_side_effects=True, vmem_limit_bytes=60 * 2**20
        ),
    )(wavefield, frequencies, velocity, bracket, *tables)


def on_device(wavefield, frequencies, velocity, bracket):
    devices = lax.axis_size("slab")
    fits = (
        wavefield.shape[0] == 1
        and velocity.shape[0] == 1
        and wavefield.shape[2] == lanes
        and wavefield.shape[3] == devices * lanes
        and devices in (4, 8, 16)
    )
    if fits:
        return migrate(devices, wavefield, frequencies, velocity, bracket)
    return per_device(wavefield, frequencies, velocity, bracket)


def solution(mesh):
    return jax.shard_map(
        on_device,
        mesh=mesh,
        in_specs=(
            P("shot", None, "slab", None),
            P("shot"),
            P(None, "slab", None),
            P(None, "slab", None),
        ),
        out_specs=(P("shot", None, "slab", None), P("shot", "slab", None)),
        check_vma=False,
    )
```

```python
import math

import jax
import jax.numpy as jnp
import ml_dtypes
import numpy as np
from jax import lax
from jax.experimental import pallas as pl
from jax.experimental.pallas import tpu as pltpu
from jax.sharding import PartitionSpec as P

ref_speeds = (1.0, 1.5, 2.25)
step_length = 1.0
highest = lax.Precision.HIGHEST


def dft_table(height, breadth, modulus, direction):
    down_index = lax.iota(jnp.int32, height)[:, None]
    across_index = lax.iota(jnp.int32, breadth)[None, :]
    angles = (down_index * across_index % modulus).astype(jnp.float32) * (
        direction * 2.0 * math.pi / modulus
    )
    return (jnp.cos(angles), jnp.sin(angles))


def contract(pattern, left_pair, right_pair):

    def product(one_side, other_side):
        return jnp.einsum(pattern, one_side, other_side, precision=highest)

    return (
        product(left_pair[0], right_pair[0]) - product(left_pair[1], right_pair[1]),
        product(left_pair[0], right_pair[1]) + product(left_pair[1], right_pair[0]),
    )


def rotate(values, factor_pair):
    return (
        values[0] * factor_pair[0] - values[1] * factor_pair[1],
        values[0] * factor_pair[1] + values[1] * factor_pair[0],
    )


def forward_lines(fields):
    item_count, row_count, extent = fields[0].shape
    devices = lax.axis_size("slab")
    line_count = extent // devices
    reshaped = tuple(
        (part_now.reshape(item_count, row_count, line_count, devices) for part_now in fields)
    )
    section_one = contract(
        "nrab,ak->nrkb", reshaped, dft_table(line_count, line_count, line_count, -1.0)
    )
    twisted = rotate(
        section_one,
        tuple((turning[None, None] for turning in dft_table(line_count, devices, extent, -1.0))),
    )
    section_two = contract("nrkb,bq->nkqr", twisted, dft_table(devices, devices, devices, -1.0))
    return tuple(
        (part_now.reshape(item_count, line_count, devices * row_count) for part_now in section_two)
    )


def forward_rows(fields):
    item_count, line_count, extent = fields[0].shape
    devices = lax.axis_size("slab")
    row_count = extent // devices
    reshaped = tuple(
        (part_now.reshape(item_count, line_count, devices, row_count) for part_now in fields)
    )
    section_one = contract("ncab,ak->nckb", reshaped, dft_table(devices, devices, devices, -1.0))
    twisted = rotate(
        section_one,
        tuple((turning[None, None] for turning in dft_table(devices, row_count, extent, -1.0))),
    )
    section_two = contract(
        "nckb,bq->nckq", twisted, dft_table(row_count, row_count, row_count, -1.0)
    )
    return tuple((part_now.reshape(item_count, line_count, extent) for part_now in section_two))


def inverse_rows(fields):
    item_count, line_count, extent = fields[0].shape
    devices = lax.axis_size("slab")
    row_count = extent // devices
    reshaped = tuple(
        (part_now.reshape(item_count, line_count, devices, row_count) for part_now in fields)
    )
    section_one = contract(
        "nckq,bq->nckb", reshaped, dft_table(row_count, row_count, row_count, 1.0)
    )
    twisted = rotate(
        section_one,
        tuple((turning[None, None] for turning in dft_table(devices, row_count, extent, 1.0))),
    )
    section_two = contract("nckb,ak->ncab", twisted, dft_table(devices, devices, devices, 1.0))
    return tuple(
        (
            part_now.reshape(item_count, line_count, extent) * (1.0 / extent)
            for part_now in section_two
        )
    )


def inverse_lines(fields):
    item_count, line_count, extent = fields[0].shape
    devices = lax.axis_size("slab")
    row_count = extent // devices
    total_lines = line_count * devices
    reshaped = tuple(
        (part_now.reshape(item_count, line_count, devices, row_count) for part_now in fields)
    )
    section_one = contract("nkqr,bq->nkbr", reshaped, dft_table(devices, devices, devices, 1.0))
    twisted = rotate(
        section_one,
        tuple(
            (
                turning[None, :, :, None]
                for turning in dft_table(line_count, devices, total_lines, 1.0)
            )
        ),
    )
    section_two = contract(
        "nkbr,ak->nrab", twisted, dft_table(line_count, line_count, line_count, 1.0)
    )
    return tuple(
        (
            part_now.reshape(item_count, row_count, total_lines) * (1.0 / total_lines)
            for part_now in section_two
        )
    )


def phase_shift(values, wave_square, angular):
    slowness = 1.0 / jnp.array(ref_speeds, jnp.float32)
    wave_number = angular[:, None] * slowness[None, :]
    vertical = (wave_number * wave_number)[:, :, None, None] - wave_square[None, None]
    root_abs = jnp.sqrt(jnp.abs(vertical))
    real_part = jnp.where(
        vertical >= 0, jnp.cos(step_length * root_abs), jnp.exp(-step_length * root_abs)
    )
    imag_part = jnp.where(vertical >= 0, jnp.sin(step_length * root_abs), 0.0)
    shifted = rotate((values[0][:, None], values[1][:, None]), (real_part, imag_part))
    item_count = values[0].shape[0]
    return tuple(
        (
            part_now.reshape((item_count * len(ref_speeds),) + values[0].shape[1:])
            for part_now in shifted
        )
    )


def weights(speed_grid, chosen):
    speeds = jnp.array(ref_speeds, jnp.float32)
    lower_speed = jnp.zeros_like(speed_grid)
    upper_speed = jnp.zeros_like(speed_grid)
    for ref_index in range(len(ref_speeds) - 1):
        lower_speed = lower_speed + jnp.where(chosen == ref_index, speeds[ref_index], 0.0)
        upper_speed = upper_speed + jnp.where(chosen == ref_index, speeds[ref_index + 1], 0.0)
    fraction = (speed_grid - lower_speed) / (upper_speed - lower_speed)
    residual_phase = 1.0 / speed_grid - ((1.0 - fraction) / lower_speed + fraction / upper_speed)
    coefficients = []
    for ref_index in range(len(ref_speeds)):
        coefficients.append(
            jnp.where(chosen == ref_index, 1.0 - fraction, 0.0)
            + jnp.where(chosen == ref_index - 1, fraction, 0.0)
        )
    return (jnp.stack(coefficients), residual_phase)


def advance(fields, angular, coefficients, residual_phase, spec_square):
    item_count, row_count, extent = fields[0].shape
    prepared = forward_lines(fields)
    spectrum = forward_rows(
        (
            lax.all_to_all(prepared[0], "slab", split_axis=2, concat_axis=2, tiled=True),
            lax.all_to_all(prepared[1], "slab", split_axis=2, concat_axis=2, tiled=True),
        )
    )
    returned = inverse_rows(phase_shift(spectrum, spec_square, angular))
    waves = inverse_lines(
        (
            lax.all_to_all(returned[0], "slab", split_axis=2, concat_axis=2, tiled=True),
            lax.all_to_all(returned[1], "slab", split_axis=2, concat_axis=2, tiled=True),
        )
    )
    ref_count = len(ref_speeds)
    wave_real = waves[0].reshape(item_count, ref_count, row_count, extent)
    wave_imag = waves[1].reshape(item_count, ref_count, row_count, extent)
    blended_real = jnp.sum(coefficients[None] * wave_real, axis=1)
    blended_imag = jnp.sum(coefficients[None] * wave_imag, axis=1)
    angles = angular[:, None, None] * step_length * residual_phase[None]
    return rotate((blended_real, blended_imag), (jnp.cos(angles), jnp.sin(angles)))


def folded(indices, modulus):
    return jnp.minimum(indices, modulus - indices).astype(jnp.float32) * (2.0 * math.pi / modulus)


def per_device(wavefield, frequencies, velocity, bracket):
    devices = lax.axis_size("slab")
    device_index = lax.axis_index("slab")
    row_count = wavefield.shape[2]
    extent_y = wavefield.shape[3]
    extent_x = row_count * devices
    line_count = extent_y // devices
    speed_columns = lax.all_to_all(velocity, "slab", split_axis=2, concat_axis=1, tiled=True)
    speed_rows = jnp.transpose(speed_columns, (0, 2, 1))
    column = lax.iota(jnp.int32, extent_x)
    line_index = lax.iota(jnp.int32, line_count)
    spec_first = folded(column // row_count + devices * (column % row_count), extent_x)
    spec_second = folded(device_index * line_count + line_index, extent_y)
    spec_square = (
        spec_first[None, :] * spec_first[None, :] + spec_second[:, None] * spec_second[:, None]
    )
    current = (wavefield[:, 0], wavefield[:, 1])
    coefficients, residual_phase = weights(speed_rows[0], bracket[0])
    single = (current[0], current[1])
    pieces = [advance(single, frequencies, coefficients, residual_phase, spec_square)]
    current = (
        jnp.concatenate([piece[0] for piece in pieces], axis=0),
        jnp.concatenate([piece[1] for piece in pieces], axis=0),
    )
    image_rows = [jnp.sum(current[0], axis=0)]
    return (jnp.stack(current, axis=1), jnp.stack(image_rows))


lanes = 128
chunk = 8
bfloat = jnp.bfloat16
phase_degree = 9


def split_tables(devices):
    extent = devices * lanes
    block = np.arange(devices)[:, None, None]
    down = np.arange(lanes)[None, :, None]
    across = np.arange(lanes)[None, None, :]
    angles = (down * (block + devices * across) % extent) * (2.0 * math.pi / extent)
    cosine, sine = np.cos(angles), np.sin(angles)
    table = np.concatenate(
        [np.concatenate([cosine, -sine], 2), np.concatenate([sine, cosine], 2)], 1
    ).astype(np.float32)
    pieces = []
    for whole in (table, np.ascontiguousarray(np.swapaxes(table, 1, 2))):
        high = whole.astype(ml_dtypes.bfloat16)
        pieces += [high, (whole - high.astype(np.float32)).astype(ml_dtypes.bfloat16)]
    return pieces


def phase_series():
    top = 9.1
    nodes = 0.5 * top * (1.0 + np.cos(math.pi * (np.arange(64) + 0.5) / 64))
    root = np.sqrt(nodes)
    out = []
    for values in (np.cos(root), np.sin(root) / root):
        fit = np.polynomial.chebyshev.Chebyshev.fit(nodes, values, phase_degree, domain=[0, top])
        out.append([float(c) for c in fit.convert(kind=np.polynomial.Polynomial).coef])
    return out


def horner(coefficients, u):
    total = jnp.full_like(u, coefficients[-1])
    for c in coefficients[-2::-1]:
        total = total * u + c
    return total


def halves(values):
    high = values.astype(bfloat)
    return high, (values - high.astype(jnp.float32)).astype(bfloat)


def dot(left, right):
    return jnp.dot(left, right, preferred_element_type=jnp.float32)


def dot_right(values, high, low):
    top, rest = halves(values)
    return dot(top, high) + (dot(rest, high) + dot(top, low))


def dot_left(high, low, values):
    top, rest = halves(values)
    return dot(high, top) + (dot(high, rest) + dot(low, top))


def turned(value, k, count, sign):
    re, im = value
    h = math.sqrt(0.5)
    if k == 0:
        return re, im
    if 4 * k == count:
        return -sign * im, sign * re
    if 8 * k == count:
        return h * (re - sign * im), h * (im + sign * re)
    if 8 * k == 3 * count:
        return -h * (re + sign * im), h * (sign * re - im)
    c = math.cos(2.0 * math.pi * k / count)
    s = sign * math.sin(2.0 * math.pi * k / count)
    return c * re - s * im, c * im + s * re


def butterflies(values, sign):
    count = len(values)
    if count == 1:
        return values
    even = butterflies(values[0::2], sign)
    odd = butterflies(values[1::2], sign)
    first, second = [], []
    for k in range(count // 2):
        er, ei = even[k]
        re, im = turned(odd[k], k, count, sign)
        first.append((er + re, ei + im))
        second.append((er - re, ei - im))
    return first + second


def half_butterflies(values, sign, side):
    count = len(values)
    even = butterflies(values[0::2], sign)
    odd = butterflies(values[1::2], sign)
    out = []
    for k in range(count // 2):
        er, ei = even[k]
        re, im = turned(odd[k], k, count, sign)
        out.append((er + side * re, ei + side * im))
    return out


def migrate_kernel(
    devices,
    wave_ref, freq_ref, vel_ref, bracket_ref, ah_ref, al_ref, th_ref, tl_ref,
    out_ref, image_ref,
    lines, sends, spec, factors, mixed, parts, waves, speed_recv, coef, turn,
    send_f, recv_f, send_v, recv_v, send_p, recv_p, send_w, recv_w,
):
    me = lax.axis_index("slab")
    refs = len(ref_speeds)
    steps = lanes // chunk
    extent = devices * lanes
    cos_series, sin_series = phase_series()

    half = devices // 2
    place = lax.rem(me, half)
    base = me - place
    other = half - base

    def forward_copy(e, target, block):
        return pltpu.make_async_remote_copy(
            src_ref=sends.at[e * half + lax.rem(target, half)], dst_ref=spec.at[e, block],
            send_sem=send_f.at[e, target], recv_sem=recv_f.at[e, block],
            device_id={"slab": target}, device_id_type=pl.DeviceIdType.MESH,
        )

    shot = lax.axis_index("shot")
    own = pl.ds(pl.multiple_of(shot * (lanes // 2), lanes // 2), lanes // 2)
    partner = {"shot": 1 - shot, "slab": me}

    def speed_swap():
        return pltpu.make_async_remote_copy(
            src_ref=speed_recv.at[:, own], dst_ref=speed_recv.at[:, own],
            send_sem=send_w, recv_sem=recv_w,
            device_id=partner, device_id_type=pl.DeviceIdType.MESH,
        )

    def speed_copy(target, block):
        return pltpu.make_async_remote_copy(
            src_ref=vel_ref.at[0, own, pl.ds(pl.multiple_of(target * lanes, lanes), lanes)],
            dst_ref=speed_recv.at[block, own],
            send_sem=send_v.at[target], recv_sem=recv_v.at[block],
            device_id={"slab": target}, device_id_type=pl.DeviceIdType.MESH,
        )

    def part_copy(j, e, target, block):
        return pltpu.make_async_remote_copy(
            src_ref=parts.at[j, e, target], dst_ref=waves.at[j, e * half + block],
            send_sem=send_p.at[j, e, target], recv_sem=recv_p.at[j, e, block],
            device_id={"slab": base + target}, device_id_type=pl.DeviceIdType.MESH,
        )

    def near(step):
        return lax.rem(place + step, half)

    def near_origin(step):
        return lax.rem(place + half - step, half)

    def peer(step):
        return lax.rem(me + step, devices)

    def origin(step):
        return lax.rem(me + devices - step, devices)

    barrier = pltpu.get_barrier_semaphore()

    @pl.loop(1, devices)
    def _(step):
        pl.semaphore_signal(
            barrier, inc=1, device_id={"slab": peer(step)}, device_id_type=pl.DeviceIdType.MESH
        )

    pl.semaphore_signal(barrier, inc=1, device_id=partner, device_id_type=pl.DeviceIdType.MESH)

    @pl.loop(0, steps)
    def _(i):
        rows = pl.ds(pl.multiple_of(i * chunk, chunk), chunk)
        values = [
            (
                wave_ref[0, 0, rows, a * lanes : (a + 1) * lanes],
                wave_ref[0, 1, rows, a * lanes : (a + 1) * lanes],
            )
            for a in range(devices)
        ]
        for k, (re, im) in enumerate(butterflies(values, -1.0)):
            lines[k, rows, :lanes] = re
            lines[k, rows, lanes:] = im

    pl.semaphore_wait(barrier, devices)

    for e in range(2):

        @pl.loop(0, half)
        def _(step):
            k = near(step)
            c = e * half + k
            got = dot_right(lines[c], ah_ref[c], al_ref[c])
            sends[c, :lanes, :] = got[:, :lanes]
            sends[c, lanes:, :] = got[:, lanes:]
            forward_copy(e, other + k, me).start()

            @pl.when(step > 0)
            def _():
                forward_copy(e, base + k, me).start()

        spec[e, me] = sends[e * half + place]

    angular = freq_ref[0]
    unit = 2.0 * math.pi / extent
    tall = 4 * chunk
    row_iota = lax.broadcasted_iota(jnp.int32, (tall, lanes), 0)
    lane_iota = lax.broadcasted_iota(jnp.int32, (tall, lanes), 1)
    scale = 1.0 / (extent * extent)
    side = (1 - 2 * (base // half)).astype(jnp.float32)

    def make_factors(e):
        line_index = e * half + place + devices * lane_iota
        second = jnp.minimum(line_index, extent - line_index).astype(jnp.float32) * unit
        second_square = second * second

        @pl.loop(0, devices)
        def _(k):
            @pl.loop(0, lanes // tall)
            def _(i):
                start = pl.multiple_of(i * tall, tall)
                column = k + devices * (row_iota + start)
                first = jnp.minimum(column, extent - column).astype(jnp.float32) * unit
                square = first * first + second_square
                for j, speed in enumerate(ref_speeds):
                    number = angular * np.float32(1.0 / speed)
                    vertical = number * number - square
                    root = jnp.sqrt(jnp.abs(vertical))
                    decayed = jnp.exp(-root)
                    real = jnp.where(vertical >= 0, horner(cos_series, vertical), decayed)
                    imag = jnp.where(vertical >= 0, root * horner(sin_series, vertical), 0.0)
                    factors[j, k, pl.ds(start, tall), :] = real * scale
                    factors[j, k, pl.ds(start + lanes, tall), :] = imag * scale

    def across(ref, out, transform):
        @pl.loop(0, steps)
        def _(i):
            top = pl.ds(pl.multiple_of(i * chunk, chunk), chunk)
            low = pl.ds(pl.multiple_of(i * chunk + lanes, chunk), chunk)
            values = [(ref[d, top, :], ref[d, low, :]) for d in range(devices)]
            for k, (re, im) in enumerate(transform(values)):
                out[k, top, :] = re
                out[k, low, :] = im

    for e in range(2):
        make_factors(e)

        @pl.loop(0, half)
        def _(step):
            k = near_origin(step)
            forward_copy(e, other + k, other + k).wait_recv()

            @pl.when(step > 0)
            def _():
                forward_copy(e, base + k, base + k).wait_recv()

        if e == 1:

            @pl.loop(1, devices)
            def _(step):
                speed_copy(peer(step), me).start()

        across(spec.at[e], spec.at[e], lambda values: butterflies(values, -1.0))

        for j in range(refs):

            @pl.loop(0, devices)
            def _(k):
                if j == 0:
                    spec[e, k] = dot_left(th_ref[k], tl_ref[k], spec[e, k])
                re, im = spec[e, k, :lanes, :], spec[e, k, lanes:, :]
                fr, fi = factors[j, k, :lanes, :], factors[j, k, lanes:, :]
                shifted = jnp.concatenate([re * fr - im * fi, re * fi + im * fr], axis=0)
                mixed[k] = dot_left(ah_ref[k], al_ref[k], shifted)

            across(mixed, parts.at[j, e], lambda values: half_butterflies(values, 1.0, side))

            @pl.loop(1, half)
            def _(step):
                part_copy(j, e, near(step), place).start()

            waves[j, e * half + place] = parts[j, e, place]

    def receive(j, e):
        @pl.loop(0, half)
        def _(step):
            block = near_origin(step)
            k = e * half + block

            @pl.when(step > 0)
            def _():
                part_copy(j, e, block, block).wait_recv()

            row = jnp.concatenate([waves[j, k, :lanes, :], waves[j, k, lanes:, :]], axis=1)
            got = dot_right(row, th_ref[k], tl_ref[k])
            waves[j, k, :lanes, :] = got[:, :lanes]
            waves[j, k, lanes:, :] = got[:, lanes:]

    speed_recv[me, own] = vel_ref[0, own, pl.ds(pl.multiple_of(me * lanes, lanes), lanes)]

    @pl.loop(1, devices)
    def _(step):
        k = origin(step)
        speed_copy(k, k).wait_recv()

    speed_swap().start()

    for j in range(refs):
        receive(j, 0)

    speed_swap().wait_recv()

    for a in range(devices):
        cols = slice(a * lanes, (a + 1) * lanes)
        speed = speed_recv[a].T
        chosen = bracket_ref[0, :, cols]
        is_low = chosen == 0
        lower = jnp.where(is_low, ref_speeds[0], ref_speeds[1])
        upper = jnp.where(is_low, ref_speeds[1], ref_speeds[2])
        fraction = (speed - lower) / (upper - lower)
        residual = 1.0 / speed - ((1.0 - fraction) / lower + fraction / upper)
        rest = 1.0 - fraction
        coef[0, :, cols] = jnp.where(is_low, rest, 0.0)
        coef[1, :, cols] = jnp.where(is_low, fraction, rest)
        coef[2, :, cols] = jnp.where(is_low, 0.0, fraction)
        angle = angular * step_length * residual
        u = angle * angle
        turn[0, :, cols] = horner([1.0, -1 / 2, 1 / 24, -1 / 720, 1 / 40320], u)
        turn[1, :, cols] = angle * horner([1.0, -1 / 6, 1 / 120, -1 / 5040], u)

    for j in range(refs):
        receive(j, 1)

        @pl.loop(0, steps)
        def _(i):
            top = pl.ds(pl.multiple_of(i * chunk, chunk), chunk)
            low = pl.ds(pl.multiple_of(i * chunk + lanes, chunk), chunk)
            values = [(waves[j, k, top, :], waves[j, k, low, :]) for k in range(devices)]
            for a, (re, im) in enumerate(butterflies(values, 1.0)):
                cols = slice(a * lanes, (a + 1) * lanes)
                weight = coef[j, top, cols]
                re, im = re * weight, im * weight
                if j > 0:
                    re = re + out_ref[0, 0, top, cols]
                    im = im + out_ref[0, 1, top, cols]
                if j == refs - 1:
                    c, s = turn[0, top, cols], turn[1, top, cols]
                    re, im = re * c - im * s, re * s + im * c
                    image_ref[0, top, cols] = re
                out_ref[0, 0, top, cols] = re
                out_ref[0, 1, top, cols] = im

    speed_swap().wait_send()

    @pl.loop(1, devices)
    def _(step):
        speed_copy(peer(step), me).wait_send()

    for e in range(2):

        @pl.loop(0, half)
        def _(step):
            k = near(step)
            forward_copy(e, other + k, me).wait_send()

            @pl.when(step > 0)
            def _():
                forward_copy(e, base + k, me).wait_send()
                for j in range(refs):
                    part_copy(j, e, k, place).wait_send()


def migrate(devices, wavefield, frequencies, velocity, bracket):
    refs = len(ref_speeds)
    tables = [jnp.asarray(piece) for piece in split_tables(devices)]
    extent = devices * lanes
    vmem = pl.BlockSpec(memory_space=pltpu.VMEM)
    half = devices // 2
    tall = 2 * lanes
    single = jnp.float32
    return pl.pallas_call(
        lambda *args: migrate_kernel(devices, *args),
        out_shape=(
            jax.ShapeDtypeStruct((1, 2, lanes, extent), single),
            jax.ShapeDtypeStruct((1, lanes, extent), single),
        ),
        in_specs=[vmem, pl.BlockSpec(memory_space=pltpu.SMEM)] + [vmem] * 6,
        out_specs=(vmem, vmem),
        scratch_shapes=[
            pltpu.VMEM((devices, lanes, tall), single),
            pltpu.VMEM((devices, tall, lanes), single),
            pltpu.VMEM((2, devices, tall, lanes), single),
            pltpu.VMEM((refs, devices, tall, lanes), single),
            pltpu.VMEM((devices, tall, lanes), single),
            pltpu.VMEM((refs, 2, half, tall, lanes), single),
            pltpu.VMEM((refs, devices, tall, lanes), single),
            pltpu.VMEM((devices, lanes, lanes), single),
            pltpu.VMEM((refs, lanes, extent), single),
            pltpu.VMEM((2, lanes, extent), single),
            pltpu.SemaphoreType.DMA((2, devices)),
            pltpu.SemaphoreType.DMA((2, devices)),
            pltpu.SemaphoreType.DMA((devices,)),
            pltpu.SemaphoreType.DMA((devices,)),
            pltpu.SemaphoreType.DMA((refs, 2, half)),
            pltpu.SemaphoreType.DMA((refs, 2, half)),
            pltpu.SemaphoreType.DMA,
            pltpu.SemaphoreType.DMA,
        ],
        compiler_params=pltpu.CompilerParams(
            collective_id=0, has_side_effects=True, vmem_limit_bytes=60 * 2**20
        ),
    )(wavefield, frequencies, velocity, bracket, *tables)


def on_device(wavefield, frequencies, velocity, bracket):
    devices = lax.axis_size("slab")
    fits = (
        wavefield.shape[0] == 1
        and velocity.shape[0] == 1
        and wavefield.shape[2] == lanes
        and wavefield.shape[3] == devices * lanes
        and devices in (4, 8, 16)
        and lax.axis_size("shot") == 2
    )
    if fits:
        return migrate(devices, wavefield, frequencies, velocity, bracket)
    return per_device(wavefield, frequencies, velocity, bracket)


def solution(mesh):
    return jax.shard_map(
        on_device,
        mesh=mesh,
        in_specs=(
            P("shot", None, "slab", None),
            P("shot"),
            P(None, "slab", None),
            P(None, "slab", None),
        ),
        out_specs=(P("shot", None, "slab", None), P("shot", "slab", None)),
        check_vma=False,
    )
```

```python
import math

import jax
import jax.numpy as jnp
import ml_dtypes
import numpy as np
from jax import lax
from jax.experimental import pallas as pl
from jax.experimental.pallas import tpu as pltpu
from jax.sharding import PartitionSpec as P

ref_speeds = (1.0, 1.5, 2.25)
step_length = 1.0
highest = lax.Precision.HIGHEST


def dft_table(height, breadth, modulus, direction):
    down_index = lax.iota(jnp.int32, height)[:, None]
    across_index = lax.iota(jnp.int32, breadth)[None, :]
    angles = (down_index * across_index % modulus).astype(jnp.float32) * (
        direction * 2.0 * math.pi / modulus
    )
    return (jnp.cos(angles), jnp.sin(angles))


def contract(pattern, left_pair, right_pair):

    def product(one_side, other_side):
        return jnp.einsum(pattern, one_side, other_side, precision=highest)

    return (
        product(left_pair[0], right_pair[0]) - product(left_pair[1], right_pair[1]),
        product(left_pair[0], right_pair[1]) + product(left_pair[1], right_pair[0]),
    )


def rotate(values, factor_pair):
    return (
        values[0] * factor_pair[0] - values[1] * factor_pair[1],
        values[0] * factor_pair[1] + values[1] * factor_pair[0],
    )


def forward_lines(fields):
    item_count, row_count, extent = fields[0].shape
    devices = lax.axis_size("slab")
    line_count = extent // devices
    reshaped = tuple(
        (part_now.reshape(item_count, row_count, line_count, devices) for part_now in fields)
    )
    section_one = contract(
        "nrab,ak->nrkb", reshaped, dft_table(line_count, line_count, line_count, -1.0)
    )
    twisted = rotate(
        section_one,
        tuple((turning[None, None] for turning in dft_table(line_count, devices, extent, -1.0))),
    )
    section_two = contract("nrkb,bq->nkqr", twisted, dft_table(devices, devices, devices, -1.0))
    return tuple(
        (part_now.reshape(item_count, line_count, devices * row_count) for part_now in section_two)
    )


def forward_rows(fields):
    item_count, line_count, extent = fields[0].shape
    devices = lax.axis_size("slab")
    row_count = extent // devices
    reshaped = tuple(
        (part_now.reshape(item_count, line_count, devices, row_count) for part_now in fields)
    )
    section_one = contract("ncab,ak->nckb", reshaped, dft_table(devices, devices, devices, -1.0))
    twisted = rotate(
        section_one,
        tuple((turning[None, None] for turning in dft_table(devices, row_count, extent, -1.0))),
    )
    section_two = contract(
        "nckb,bq->nckq", twisted, dft_table(row_count, row_count, row_count, -1.0)
    )
    return tuple((part_now.reshape(item_count, line_count, extent) for part_now in section_two))


def inverse_rows(fields):
    item_count, line_count, extent = fields[0].shape
    devices = lax.axis_size("slab")
    row_count = extent // devices
    reshaped = tuple(
        (part_now.reshape(item_count, line_count, devices, row_count) for part_now in fields)
    )
    section_one = contract(
        "nckq,bq->nckb", reshaped, dft_table(row_count, row_count, row_count, 1.0)
    )
    twisted = rotate(
        section_one,
        tuple((turning[None, None] for turning in dft_table(devices, row_count, extent, 1.0))),
    )
    section_two = contract("nckb,ak->ncab", twisted, dft_table(devices, devices, devices, 1.0))
    return tuple(
        (
            part_now.reshape(item_count, line_count, extent) * (1.0 / extent)
            for part_now in section_two
        )
    )


def inverse_lines(fields):
    item_count, line_count, extent = fields[0].shape
    devices = lax.axis_size("slab")
    row_count = extent // devices
    total_lines = line_count * devices
    reshaped = tuple(
        (part_now.reshape(item_count, line_count, devices, row_count) for part_now in fields)
    )
    section_one = contract("nkqr,bq->nkbr", reshaped, dft_table(devices, devices, devices, 1.0))
    twisted = rotate(
        section_one,
        tuple(
            (
                turning[None, :, :, None]
                for turning in dft_table(line_count, devices, total_lines, 1.0)
            )
        ),
    )
    section_two = contract(
        "nkbr,ak->nrab", twisted, dft_table(line_count, line_count, line_count, 1.0)
    )
    return tuple(
        (
            part_now.reshape(item_count, row_count, total_lines) * (1.0 / total_lines)
            for part_now in section_two
        )
    )


def phase_shift(values, wave_square, angular):
    slowness = 1.0 / jnp.array(ref_speeds, jnp.float32)
    wave_number = angular[:, None] * slowness[None, :]
    vertical = (wave_number * wave_number)[:, :, None, None] - wave_square[None, None]
    root_abs = jnp.sqrt(jnp.abs(vertical))
    real_part = jnp.where(
        vertical >= 0, jnp.cos(step_length * root_abs), jnp.exp(-step_length * root_abs)
    )
    imag_part = jnp.where(vertical >= 0, jnp.sin(step_length * root_abs), 0.0)
    shifted = rotate((values[0][:, None], values[1][:, None]), (real_part, imag_part))
    item_count = values[0].shape[0]
    return tuple(
        (
            part_now.reshape((item_count * len(ref_speeds),) + values[0].shape[1:])
            for part_now in shifted
        )
    )


def weights(speed_grid, chosen):
    speeds = jnp.array(ref_speeds, jnp.float32)
    lower_speed = jnp.zeros_like(speed_grid)
    upper_speed = jnp.zeros_like(speed_grid)
    for ref_index in range(len(ref_speeds) - 1):
        lower_speed = lower_speed + jnp.where(chosen == ref_index, speeds[ref_index], 0.0)
        upper_speed = upper_speed + jnp.where(chosen == ref_index, speeds[ref_index + 1], 0.0)
    fraction = (speed_grid - lower_speed) / (upper_speed - lower_speed)
    residual_phase = 1.0 / speed_grid - ((1.0 - fraction) / lower_speed + fraction / upper_speed)
    coefficients = []
    for ref_index in range(len(ref_speeds)):
        coefficients.append(
            jnp.where(chosen == ref_index, 1.0 - fraction, 0.0)
            + jnp.where(chosen == ref_index - 1, fraction, 0.0)
        )
    return (jnp.stack(coefficients), residual_phase)


def advance(fields, angular, coefficients, residual_phase, spec_square):
    item_count, row_count, extent = fields[0].shape
    prepared = forward_lines(fields)
    spectrum = forward_rows(
        (
            lax.all_to_all(prepared[0], "slab", split_axis=2, concat_axis=2, tiled=True),
            lax.all_to_all(prepared[1], "slab", split_axis=2, concat_axis=2, tiled=True),
        )
    )
    returned = inverse_rows(phase_shift(spectrum, spec_square, angular))
    waves = inverse_lines(
        (
            lax.all_to_all(returned[0], "slab", split_axis=2, concat_axis=2, tiled=True),
            lax.all_to_all(returned[1], "slab", split_axis=2, concat_axis=2, tiled=True),
        )
    )
    ref_count = len(ref_speeds)
    wave_real = waves[0].reshape(item_count, ref_count, row_count, extent)
    wave_imag = waves[1].reshape(item_count, ref_count, row_count, extent)
    blended_real = jnp.sum(coefficients[None] * wave_real, axis=1)
    blended_imag = jnp.sum(coefficients[None] * wave_imag, axis=1)
    angles = angular[:, None, None] * step_length * residual_phase[None]
    return rotate((blended_real, blended_imag), (jnp.cos(angles), jnp.sin(angles)))


def folded(indices, modulus):
    return jnp.minimum(indices, modulus - indices).astype(jnp.float32) * (2.0 * math.pi / modulus)


def per_device(wavefield, frequencies, velocity, bracket):
    devices = lax.axis_size("slab")
    device_index = lax.axis_index("slab")
    row_count = wavefield.shape[2]
    extent_y = wavefield.shape[3]
    extent_x = row_count * devices
    line_count = extent_y // devices
    speed_columns = lax.all_to_all(velocity, "slab", split_axis=2, concat_axis=1, tiled=True)
    speed_rows = jnp.transpose(speed_columns, (0, 2, 1))
    column = lax.iota(jnp.int32, extent_x)
    line_index = lax.iota(jnp.int32, line_count)
    spec_first = folded(column // row_count + devices * (column % row_count), extent_x)
    spec_second = folded(device_index * line_count + line_index, extent_y)
    spec_square = (
        spec_first[None, :] * spec_first[None, :] + spec_second[:, None] * spec_second[:, None]
    )
    current = (wavefield[:, 0], wavefield[:, 1])
    coefficients, residual_phase = weights(speed_rows[0], bracket[0])
    single = (current[0], current[1])
    pieces = [advance(single, frequencies, coefficients, residual_phase, spec_square)]
    current = (
        jnp.concatenate([piece[0] for piece in pieces], axis=0),
        jnp.concatenate([piece[1] for piece in pieces], axis=0),
    )
    image_rows = [jnp.sum(current[0], axis=0)]
    return (jnp.stack(current, axis=1), jnp.stack(image_rows))


lanes = 128
chunk = 8
bfloat = jnp.bfloat16
phase_degree = 9


def split_tables(devices):
    extent = devices * lanes
    block = np.arange(devices)[:, None, None]
    down = np.arange(lanes)[None, :, None]
    across = np.arange(lanes)[None, None, :]
    angles = (down * (block + devices * across) % extent) * (2.0 * math.pi / extent)
    cosine, sine = np.cos(angles), np.sin(angles)
    table = np.concatenate(
        [np.concatenate([cosine, -sine], 2), np.concatenate([sine, cosine], 2)], 1
    ).astype(np.float32)
    pieces = []
    for whole in (table, np.ascontiguousarray(np.swapaxes(table, 1, 2))):
        high = whole.astype(ml_dtypes.bfloat16)
        pieces += [high, (whole - high.astype(np.float32)).astype(ml_dtypes.bfloat16)]
    return pieces


def phase_series():
    top = 9.1
    nodes = 0.5 * top * (1.0 + np.cos(math.pi * (np.arange(64) + 0.5) / 64))
    root = np.sqrt(nodes)
    out = []
    for values in (np.cos(root), np.sin(root) / root):
        fit = np.polynomial.chebyshev.Chebyshev.fit(nodes, values, phase_degree, domain=[0, top])
        out.append([float(c) for c in fit.convert(kind=np.polynomial.Polynomial).coef])
    return out


def horner(coefficients, u):
    total = jnp.full_like(u, coefficients[-1])
    for c in coefficients[-2::-1]:
        total = total * u + c
    return total


def halves(values):
    high = values.astype(bfloat)
    return high, (values - high.astype(jnp.float32)).astype(bfloat)


def dot(left, right):
    return jnp.dot(left, right, preferred_element_type=jnp.float32)


def dot_right(values, high, low):
    top, rest = halves(values)
    return dot(top, high) + (dot(rest, high) + dot(top, low))


def dot_left(high, low, values):
    top, rest = halves(values)
    return dot(high, top) + (dot(high, rest) + dot(low, top))


def turned(value, k, count, sign):
    re, im = value
    h = math.sqrt(0.5)
    if k == 0:
        return re, im
    if 4 * k == count:
        return -sign * im, sign * re
    if 8 * k == count:
        return h * (re - sign * im), h * (im + sign * re)
    if 8 * k == 3 * count:
        return -h * (re + sign * im), h * (sign * re - im)
    c = math.cos(2.0 * math.pi * k / count)
    s = sign * math.sin(2.0 * math.pi * k / count)
    return c * re - s * im, c * im + s * re


def butterflies(values, sign):
    count = len(values)
    if count == 1:
        return values
    even = butterflies(values[0::2], sign)
    odd = butterflies(values[1::2], sign)
    first, second = [], []
    for k in range(count // 2):
        er, ei = even[k]
        re, im = turned(odd[k], k, count, sign)
        first.append((er + re, ei + im))
        second.append((er - re, ei - im))
    return first + second


def half_butterflies(values, sign, side):
    count = len(values)
    even = butterflies(values[0::2], sign)
    odd = butterflies(values[1::2], sign)
    out = []
    for k in range(count // 2):
        er, ei = even[k]
        re, im = turned(odd[k], k, count, sign)
        out.append((er + side * re, ei + side * im))
    return out


def migrate_kernel(
    devices,
    wave_ref, freq_ref, vel_ref, bracket_ref, ah_ref, al_ref, th_ref, tl_ref,
    real_ref, imag_ref,
    lines, sends, spec, factors, mixed, parts, waves, speed_recv, coef, turn,
    send_f, recv_f, send_v, recv_v, send_p, recv_p, send_w, recv_w,
):
    me = lax.axis_index("slab")
    refs = len(ref_speeds)
    steps = lanes // chunk
    extent = devices * lanes
    cos_series, sin_series = phase_series()

    half = devices // 2
    place = lax.rem(me, half)
    base = me - place
    other = half - base

    def forward_copy(e, target, block):
        return pltpu.make_async_remote_copy(
            src_ref=sends.at[e * half + lax.rem(target, half)], dst_ref=spec.at[e, block],
            send_sem=send_f.at[e, target], recv_sem=recv_f.at[e, block],
            device_id={"slab": target}, device_id_type=pl.DeviceIdType.MESH,
        )

    shot = lax.axis_index("shot")
    own = pl.ds(pl.multiple_of(shot * (lanes // 2), lanes // 2), lanes // 2)
    partner = {"shot": 1 - shot, "slab": me}

    def speed_swap():
        return pltpu.make_async_remote_copy(
            src_ref=speed_recv.at[:, own], dst_ref=speed_recv.at[:, own],
            send_sem=send_w, recv_sem=recv_w,
            device_id=partner, device_id_type=pl.DeviceIdType.MESH,
        )

    def speed_copy(target, block):
        return pltpu.make_async_remote_copy(
            src_ref=vel_ref.at[0, own, pl.ds(pl.multiple_of(target * lanes, lanes), lanes)],
            dst_ref=speed_recv.at[block, own],
            send_sem=send_v.at[target], recv_sem=recv_v.at[block],
            device_id={"slab": target}, device_id_type=pl.DeviceIdType.MESH,
        )

    def part_copy(j, e, target, block):
        return pltpu.make_async_remote_copy(
            src_ref=parts.at[j, e, target], dst_ref=waves.at[j, e * half + block],
            send_sem=send_p.at[j, e, target], recv_sem=recv_p.at[j, e, block],
            device_id={"slab": base + target}, device_id_type=pl.DeviceIdType.MESH,
        )

    def near(step):
        return lax.rem(place + step, half)

    def near_origin(step):
        return lax.rem(place + half - step, half)

    def peer(step):
        return lax.rem(me + step, devices)

    def origin(step):
        return lax.rem(me + devices - step, devices)

    barrier = pltpu.get_barrier_semaphore()

    @pl.loop(1, devices)
    def _(step):
        pl.semaphore_signal(
            barrier, inc=1, device_id={"slab": peer(step)}, device_id_type=pl.DeviceIdType.MESH
        )

    pl.semaphore_signal(barrier, inc=1, device_id=partner, device_id_type=pl.DeviceIdType.MESH)

    @pl.loop(0, steps)
    def _(i):
        rows = pl.ds(pl.multiple_of(i * chunk, chunk), chunk)
        values = [
            (
                wave_ref[0, 0, rows, a * lanes : (a + 1) * lanes],
                wave_ref[0, 1, rows, a * lanes : (a + 1) * lanes],
            )
            for a in range(devices)
        ]
        for k, (re, im) in enumerate(butterflies(values, -1.0)):
            lines[k, rows, :lanes] = re
            lines[k, rows, lanes:] = im

    pl.semaphore_wait(barrier, devices)

    for e in range(2):

        @pl.loop(0, half)
        def _(step):
            k = near(step)
            c = e * half + k
            got = dot_right(lines[c], ah_ref[c], al_ref[c])
            sends[c, :lanes, :] = got[:, :lanes]
            sends[c, lanes:, :] = got[:, lanes:]
            forward_copy(e, other + k, me).start()

            @pl.when(step > 0)
            def _():
                forward_copy(e, base + k, me).start()

        spec[e, me] = sends[e * half + place]

    angular = freq_ref[0]
    unit = 2.0 * math.pi / extent
    tall = 4 * chunk
    row_iota = lax.broadcasted_iota(jnp.int32, (tall, lanes), 0)
    lane_iota = lax.broadcasted_iota(jnp.int32, (tall, lanes), 1)
    scale = 1.0 / (extent * extent)
    side = (1 - 2 * (base // half)).astype(jnp.float32)

    def make_factors(e):
        line_index = e * half + place + devices * lane_iota
        second = jnp.minimum(line_index, extent - line_index).astype(jnp.float32) * unit
        second_square = second * second

        @pl.loop(0, devices)
        def _(k):
            @pl.loop(0, lanes // tall)
            def _(i):
                start = pl.multiple_of(i * tall, tall)
                column = k + devices * (row_iota + start)
                first = jnp.minimum(column, extent - column).astype(jnp.float32) * unit
                square = first * first + second_square
                for j, speed in enumerate(ref_speeds):
                    number = angular * np.float32(1.0 / speed)
                    vertical = number * number - square
                    root = jnp.sqrt(jnp.abs(vertical))
                    decayed = jnp.exp(-root)
                    real = jnp.where(vertical >= 0, horner(cos_series, vertical), decayed)
                    imag = jnp.where(vertical >= 0, root * horner(sin_series, vertical), 0.0)
                    factors[j, k, pl.ds(start, tall), :] = real * scale
                    factors[j, k, pl.ds(start + lanes, tall), :] = imag * scale

    def across(ref, out, transform):
        @pl.loop(0, steps)
        def _(i):
            top = pl.ds(pl.multiple_of(i * chunk, chunk), chunk)
            low = pl.ds(pl.multiple_of(i * chunk + lanes, chunk), chunk)
            values = [(ref[d, top, :], ref[d, low, :]) for d in range(devices)]
            for k, (re, im) in enumerate(transform(values)):
                out[k, top, :] = re
                out[k, low, :] = im

    for e in range(2):
        make_factors(e)

        @pl.loop(0, half)
        def _(step):
            k = near_origin(step)
            forward_copy(e, other + k, other + k).wait_recv()

            @pl.when(step > 0)
            def _():
                forward_copy(e, base + k, base + k).wait_recv()

        if e == 1:

            @pl.loop(1, devices)
            def _(step):
                speed_copy(peer(step), me).start()

        across(spec.at[e], spec.at[e], lambda values: butterflies(values, -1.0))

        for j in range(refs):

            @pl.loop(0, devices)
            def _(k):
                if j == 0:
                    spec[e, k] = dot_left(th_ref[k], tl_ref[k], spec[e, k])
                re, im = spec[e, k, :lanes, :], spec[e, k, lanes:, :]
                fr, fi = factors[j, k, :lanes, :], factors[j, k, lanes:, :]
                shifted = jnp.concatenate([re * fr - im * fi, re * fi + im * fr], axis=0)
                mixed[k] = dot_left(ah_ref[k], al_ref[k], shifted)

            across(mixed, parts.at[j, e], lambda values: half_butterflies(values, 1.0, side))

            @pl.loop(1, half)
            def _(step):
                part_copy(j, e, near(step), place).start()

            waves[j, e * half + place] = parts[j, e, place]

    def receive(j, e):
        @pl.loop(0, half)
        def _(step):
            block = near_origin(step)
            k = e * half + block

            @pl.when(step > 0)
            def _():
                part_copy(j, e, block, block).wait_recv()

            row = jnp.concatenate([waves[j, k, :lanes, :], waves[j, k, lanes:, :]], axis=1)
            got = dot_right(row, th_ref[k], tl_ref[k])
            waves[j, k, :lanes, :] = got[:, :lanes]
            waves[j, k, lanes:, :] = got[:, lanes:]

    speed_recv[me, own] = vel_ref[0, own, pl.ds(pl.multiple_of(me * lanes, lanes), lanes)]

    @pl.loop(1, devices)
    def _(step):
        k = origin(step)
        speed_copy(k, k).wait_recv()

    speed_swap().start()

    for j in range(refs):
        receive(j, 0)

    speed_swap().wait_recv()

    for a in range(devices):
        cols = slice(a * lanes, (a + 1) * lanes)
        speed = speed_recv[a].T
        chosen = bracket_ref[0, :, cols]
        is_low = chosen == 0
        lower = jnp.where(is_low, ref_speeds[0], ref_speeds[1])
        upper = jnp.where(is_low, ref_speeds[1], ref_speeds[2])
        fraction = (speed - lower) / (upper - lower)
        residual = 1.0 / speed - ((1.0 - fraction) / lower + fraction / upper)
        rest = 1.0 - fraction
        coef[0, :, cols] = jnp.where(is_low, rest, 0.0)
        coef[1, :, cols] = jnp.where(is_low, fraction, rest)
        coef[2, :, cols] = jnp.where(is_low, 0.0, fraction)
        angle = angular * step_length * residual
        u = angle * angle
        turn[0, :, cols] = horner([1.0, -1 / 2, 1 / 24, -1 / 720, 1 / 40320], u)
        turn[1, :, cols] = angle * horner([1.0, -1 / 6, 1 / 120, -1 / 5040], u)

    for j in range(refs):
        receive(j, 1)

        @pl.loop(0, steps)
        def _(i):
            top = pl.ds(pl.multiple_of(i * chunk, chunk), chunk)
            low = pl.ds(pl.multiple_of(i * chunk + lanes, chunk), chunk)
            values = [(waves[j, k, top, :], waves[j, k, low, :]) for k in range(devices)]
            for a, (re, im) in enumerate(butterflies(values, 1.0)):
                cols = slice(a * lanes, (a + 1) * lanes)
                weight = coef[j, top, cols]
                re, im = re * weight, im * weight
                if j > 0:
                    re = re + real_ref[0, top, cols]
                    im = im + imag_ref[0, top, cols]
                if j == refs - 1:
                    c, s = turn[0, top, cols], turn[1, top, cols]
                    re, im = re * c - im * s, re * s + im * c
                real_ref[0, top, cols] = re
                imag_ref[0, top, cols] = im

    speed_swap().wait_send()

    @pl.loop(1, devices)
    def _(step):
        speed_copy(peer(step), me).wait_send()

    for e in range(2):

        @pl.loop(0, half)
        def _(step):
            k = near(step)
            forward_copy(e, other + k, me).wait_send()

            @pl.when(step > 0)
            def _():
                forward_copy(e, base + k, me).wait_send()
                for j in range(refs):
                    part_copy(j, e, k, place).wait_send()


def migrate(devices, wavefield, frequencies, velocity, bracket):
    refs = len(ref_speeds)
    tables = [jnp.asarray(piece) for piece in split_tables(devices)]
    extent = devices * lanes
    vmem = pl.BlockSpec(memory_space=pltpu.VMEM)
    half = devices // 2
    tall = 2 * lanes
    single = jnp.float32
    real, imag = pl.pallas_call(
        lambda *args: migrate_kernel(devices, *args),
        out_shape=(
            jax.ShapeDtypeStruct((1, lanes, extent), single),
            jax.ShapeDtypeStruct((1, lanes, extent), single),
        ),
        in_specs=[vmem, pl.BlockSpec(memory_space=pltpu.SMEM)] + [vmem] * 6,
        out_specs=(vmem, vmem),
        scratch_shapes=[
            pltpu.VMEM((devices, lanes, tall), single),
            pltpu.VMEM((devices, tall, lanes), single),
            pltpu.VMEM((2, devices, tall, lanes), single),
            pltpu.VMEM((refs, devices, tall, lanes), single),
            pltpu.VMEM((devices, tall, lanes), single),
            pltpu.VMEM((refs, 2, half, tall, lanes), single),
            pltpu.VMEM((refs, devices, tall, lanes), single),
            pltpu.VMEM((devices, lanes, lanes), single),
            pltpu.VMEM((refs, lanes, extent), single),
            pltpu.VMEM((2, lanes, extent), single),
            pltpu.SemaphoreType.DMA((2, devices)),
            pltpu.SemaphoreType.DMA((2, devices)),
            pltpu.SemaphoreType.DMA((devices,)),
            pltpu.SemaphoreType.DMA((devices,)),
            pltpu.SemaphoreType.DMA((refs, 2, half)),
            pltpu.SemaphoreType.DMA((refs, 2, half)),
            pltpu.SemaphoreType.DMA,
            pltpu.SemaphoreType.DMA,
        ],
        compiler_params=pltpu.CompilerParams(
            collective_id=0, has_side_effects=True, vmem_limit_bytes=60 * 2**20
        ),
    )(wavefield, frequencies, velocity, bracket, *tables)
    return jnp.stack((real, imag), axis=1), real


def on_device(wavefield, frequencies, velocity, bracket):
    devices = lax.axis_size("slab")
    fits = (
        wavefield.shape[0] == 1
        and velocity.shape[0] == 1
        and wavefield.shape[2] == lanes
        and wavefield.shape[3] == devices * lanes
        and devices in (4, 8, 16)
        and lax.axis_size("shot") == 2
    )
    if fits:
        return migrate(devices, wavefield, frequencies, velocity, bracket)
    return per_device(wavefield, frequencies, velocity, bracket)


def solution(mesh):
    return jax.shard_map(
        on_device,
        mesh=mesh,
        in_specs=(
            P("shot", None, "slab", None),
            P("shot"),
            P(None, "slab", None),
            P(None, "slab", None),
        ),
        out_specs=(P("shot", None, "slab", None), P("shot", "slab", None)),
        check_vma=False,
    )
```
